128 devices in a mesh: occ: 8 (over z_hi, x), vir: 16 (over z_lo, y, core).
Axes of the slice: x: 4, y: 4, z: 4 (z_hi: 2, z_lo: 2; z = z_hi * 2 + z_lo), core: 2. Of those that a mesh axis runs over, the one named last changes fastest.
Arguments:
- amplitudes: bfloat16 [4096, 32, 2048], P(('occ', 'vir')), may hold values from -6 to 6
- cycle_inter: bfloat16 [2048, 2048], P(None, ('occ', 'vir')), may hold values from -0.125 to 0.125
- ladder_slab: bfloat16 [32, 256, 2048], P(None, None, 'vir'), may hold values from -0.0625 to 0.0625
- irrep_counts: int32 [8], replicated, may hold values from 144 to 256, as said below
- slab_irrep: int32 [1], replicated, may hold values from 1 to 7
Outputs:
- ladder: bfloat16 [4096, 2048], P('occ', 'vir')
The draws below stay inside these ranges and needn't reach their ends.
Inputs may be any that keep to these rules, and one draw needn't show every extreme that they name: `irrep_counts`: the counts sum to 1600.
All inputs are finite; a program needn't handle non-finite values.
Results may differ from the reference program's by a relative error of at most 0.0049.
Values may be sent and summed in bfloat16 or wider, within the bound.
A program may use at most 128 MiB of HBM per device.

```python
import jax
import jax.numpy as jnp
from jax import lax

NV = 1600
BLK = 256
CW = 32
PAIR_DEV = 32
VP = 2048
PAIRS = 4096
N_OCC = 8
N_VIR = 16


def draw_irrep_counts(key, part):
    key = jax.random.fold_in(key, 17)
    base_count = NV // 8
    reach_most = BLK - base_count
    shifted_by = jax.random.randint(jax.random.fold_in(key, 1), (4,), 0, reach_most + 1, dtype=jnp.int32)
    shifted_by = shifted_by.at[0].set(reach_most)
    counts = base_count + jnp.stack([shifted_by, -shifted_by], axis=1).reshape(8)
    return jax.random.permutation(jax.random.fold_in(key, 2), counts).astype(jnp.int32)


def levels(key, dims, cuts, low, top_value):
    def one(axis_at, shards_of):
        heights = jax.random.uniform(jax.random.fold_in(jax.random.fold_in(key, 6), axis_at), (shards_of,), jnp.float32, low / len(cuts), top_value / len(cuts))
        return jnp.repeat(jnp.exp(heights), dims[axis_at] // shards_of).reshape((-1,) + (1,) * (len(dims) - axis_at - 1))

    gain = one(*cuts[0])
    for cut in cuts[1:]:
        gain = gain * one(*cut)
    return gain


def noise(own_key, extent, deviation, reach, split=(), kind=jnp.bfloat16):
    array = jax.random.normal(own_key, extent, jnp.float32) * deviation
    if len(split) > 0:
        array = levels(own_key, extent, split, -0.22, 0.18) * array
    return jnp.clip(array, min=-reach, max=reach).astype(kind)


def setup_inputs(seed: int = 0) -> dict:
    arg_keys = jax.random.split(jax.random.key(seed), 6)
    amplitudes = noise(arg_keys[0], (PAIRS, CW, VP), 1.0, 6.0, ((0, 128),))
    cycle_inter = noise(arg_keys[1], (VP, VP), VP ** -0.5, 0.125, ((1, 128),))
    ladder_slab = noise(arg_keys[2], (CW, BLK, VP), (CW * BLK) ** -0.5, 0.0625, ((2, 16),))
    irrep_counts = draw_irrep_counts(jax.random.fold_in(arg_keys[5], 71), 0)
    slab_irrep = jax.random.randint(arg_keys[4], (1,), 1, 8).astype(jnp.int32)
    return {"amplitudes": amplitudes, "cycle_inter": cycle_inter, "ladder_slab": ladder_slab, "irrep_counts": irrep_counts, "slab_irrep": slab_irrep}


def live_columns(irrep_counts, first_col, col_count):
    col_index = first_col + jnp.arange(col_count, dtype=jnp.int32)
    block_of = col_index // BLK
    matches = block_of[:, None] == jnp.arange(8, dtype=jnp.int32)[None, :]
    live_bound = jnp.sum(jnp.where(matches, irrep_counts[None, :], 0), axis=1)
    return (col_index % BLK < live_bound).astype(jnp.float32)


def reference(amplitudes, cycle_inter, ladder_slab, irrep_counts, slab_irrep):
    live_cols = live_columns(irrep_counts, 0, VP)
    block_order = jnp.bitwise_xor(jnp.arange(8, dtype=jnp.int32), slab_irrep[0])
    weights = ladder_slab.astype(jnp.float32).reshape(CW, BLK, 8, BLK)

    def one_group(group_amps):
        masked = jnp.where(live_cols > 0, group_amps, jnp.zeros_like(group_amps))
        flattened = masked.reshape(-1, VP)
        dressed = flattened.astype(jnp.float32) + jnp.dot(flattened, cycle_inter, preferred_element_type=jnp.float32)
        dressed = (dressed * live_cols).astype(jnp.bfloat16)
        blocks = dressed.reshape(-1, CW, 8, BLK)
        paired = jnp.take(blocks, block_order, axis=2).astype(jnp.float32)
        summed = jnp.einsum("pchl,clhm->phm", paired, weights).reshape(-1, VP)
        return (summed * live_cols).astype(jnp.bfloat16)

    grouped = amplitudes.reshape(N_OCC, PAIR_DEV * N_VIR, CW, VP)
    return lax.map(one_group, grouped).reshape(PAIRS, VP)
```

```python
import jax
import jax.numpy as jnp
from jax import lax
from jax.experimental import pallas as pl
from jax.experimental.pallas import tpu as pltpu
from jax.sharding import PartitionSpec as P

BLK = 256
WIDTHS = (768, 640, 640)
ORDERS = ("yzx", "zxy", "xyz")
NR = 4
MESH = pl.DeviceIdType.MESH
F32 = jnp.float32
BF16 = jnp.bfloat16
ALL = slice(None)


def device(x, y, z, core):
    return (z // 2 * 4 + x, z % 2 * 8 + y * 2 + core)


def kernel(
    amp_hbm, cyc_hbm, slab_hbm, counts, table, out_ref,
    raw, trans, amp, g0, g1, g2, dressed, recv, slab, total, mine, theirs,
    local_sem, gather_send, gather_recv, sib_send, sib_recv, a2a_send, a2a_recv, fin_sem,
):
    occ, vir = lax.axis_index("occ"), lax.axis_index("vir")
    x, y, core = occ % 4, vir // 2 % 4, vir % 2
    zh, zl = occ // 4, vir // 8
    z = zh * 2 + zl
    my_h = vir // 2
    gs = (g0, g1, g2)
    pos = {"x": x, "y": y, "z": z}
    sibling = device(x, y, z, 1 - core)

    def neighbour(dim, step):
        at = dict(pos)
        at[dim] = (at[dim] + step) % 4
        return device(at["x"], at["y"], at["z"], core)

    load_amp = pltpu.make_async_copy(amp_hbm, raw, local_sem.at[0])
    load_amp.start()
    half = pl.ds(pl.multiple_of(core * 128, 128), 128)
    load_slab = pltpu.make_async_copy(slab_hbm, slab.at[:, :, half], local_sem.at[1])
    load_slab.start()
    offset = 0
    load_cyc = []
    for p in range(3):
        w = WIDTHS[p]
        load_cyc.append(
            pltpu.make_async_copy(
                cyc_hbm.at[:, pl.ds(offset, w)], gs[p].at[zh, x, zl, y, core], local_sem.at[2 + p]
            )
        )
        load_cyc[-1].start()
        offset += w

    barrier = pltpu.get_barrier_semaphore()
    peers = [((my_h // 4 + j // 4) % 2) * 4 + (my_h + j) % 4 for j in range(8)]
    greet = [sibling, neighbour("x", 1), neighbour("x", 3)]
    outer_z = (z + 3 + 2 * zl) % 4
    greet.append(device(x, y, outer_z, core))
    greet += [(occ, peers[j] * 2 + core) for j in range(1, 8)]
    for who in greet:
        pl.semaphore_signal(barrier, inc=1, device_id=who, device_id_type=MESH)
    pl.semaphore_wait(barrier, len(greet))

    def region(p, phase, k, part):
        done = ORDERS[p][:phase]
        dim = ORDERS[p][phase]
        at = {}
        for name in "xyz":
            at[name] = ALL if name in done else pos[name]
        at[dim] = k
        zhi, zlo = (ALL, ALL) if "z" in done else (at["z"] // 2, at["z"] % 2)
        xs, ys = at["x"], at["y"]
        if part is not None and phase > 0:
            if "z" in done:
                zhi = part
            elif "x" in done:
                xs = pl.ds(2 * part, 2)
            else:
                ys = pl.ds(2 * part, 2)
        return gs[p].at[zhi, xs, zlo, ys, core]

    def piece(p, phase, k, part, slot, who):
        ref = region(p, phase, k, part)
        return pltpu.make_async_remote_copy(
            src_ref=ref, dst_ref=ref,
            send_sem=gather_send.at[p, phase, slot], recv_sem=gather_recv.at[p, phase, slot],
            device_id=who, device_id_type=MESH,
        )

    def to_sibling(p, ref, slot):
        return pltpu.make_async_remote_copy(
            src_ref=ref, dst_ref=ref,
            send_sem=sib_send.at[p, slot], recv_sem=sib_recv.at[p, slot],
            device_id=sibling, device_id_type=MESH,
        )

    def sib_wait(p, ref_of, slot):
        ref = ref_of
        return pltpu.make_async_remote_copy(
            src_ref=ref, dst_ref=ref,
            send_sem=sib_send.at[p, slot], recv_sem=sib_recv.at[p, slot],
            device_id=sibling, device_id_type=MESH,
        )

    sent = []

    def go(copy):
        copy.start()
        sent.append(copy)

    lane = lax.broadcasted_iota(jnp.int32, (1, BLK), 1)

    def transpose_block(k):
        cols = pl.ds(pl.multiple_of(k * BLK, BLK), BLK)
        block = raw[:, :, cols].astype(F32)
        block = jnp.where((lane < counts[k])[None], block, 0.0)
        block = block.reshape(1024, BLK)
        trans[0] = block[:, :128]
        trans[1] = block[:, 128:]

        def one(c, carry):
            rows = pl.ds(c, 32, stride=32)
            pair = [trans[0, rows, :], trans[1, rows, :]]
            amp[k, c] = jnp.concatenate(pair, axis=1).astype(BF16)
            return carry

        lax.fori_loop(0, 32, one, 0, unroll=4)

    def transpose_blocks(first, last):
        def one(k, carry):
            transpose_block(k)
            return carry

        lax.fori_loop(first, last, one, 0)

    load_slab.wait()
    slab_copy = pltpu.make_async_remote_copy(
        src_ref=slab.at[:, :, half], dst_ref=slab.at[:, :, half],
        send_sem=fin_sem.at[0], recv_sem=fin_sem.at[1],
        device_id=sibling, device_id_type=MESH,
    )

    for phase in range(3):
        for p in range(3):
            dim = ORDERS[p][phase]
            k = pos[dim]
            right, left = neighbour(dim, 1), neighbour(dim, 3)
            if phase == 0:
                load_cyc[p].wait()
                go(piece(p, phase, k, None, 0, right))
                go(piece(p, phase, k, None, 1, left))
            else:
                go(piece(p, phase, k, 0, 0, right))
                go(piece(p, phase, k, 1, 1, left))
                go(piece(p, phase, k, 1, 2, right))
                go(piece(p, phase, k, 0, 3, left))
        if phase == 0:
            slab_copy.start()
            load_amp.wait()
            transpose_blocks(0, 1)
        if phase == 1:
            transpose_blocks(1, 3)
        if phase == 2:
            for p in range(3):
                dim = ORDERS[p][2]
                go(to_sibling(p, region(p, 2, pos[dim], None), 0))
            transpose_blocks(3, 8)
        for p in range(3):
            dim = ORDERS[p][phase]
            k = pos[dim]
            right, left = neighbour(dim, 1), neighbour(dim, 3)
            before, after = (k + 3) % 4, (k + 1) % 4
            if phase == 0:
                piece(p, phase, before, None, 0, right).wait_recv()
                piece(p, phase, after, None, 1, left).wait_recv()
                if p == 1:
                    go(piece(p, phase, after, None, 4, left))
                else:
                    go(piece(p, phase, before, None, 4, right))
            else:
                piece(p, phase, before, 0, 0, right).wait_recv()
                go(piece(p, phase, before, 0, 4, right))
                piece(p, phase, after, 1, 1, left).wait_recv()
                go(piece(p, phase, after, 1, 5, left))
        for p in range(3):
            dim = ORDERS[p][phase]
            k = pos[dim]
            right, left = neighbour(dim, 1), neighbour(dim, 3)
            before, after, far = (k + 3) % 4, (k + 1) % 4, (k + 2) % 4
            if phase > 0:
                piece(p, phase, before, 1, 2, right).wait_recv()
                piece(p, phase, after, 0, 3, left).wait_recv()
            if phase == 2:
                go(to_sibling(p, region(p, 2, before, None), 1))
                go(to_sibling(p, region(p, 2, after, None), 2))
        for p in range(3):
            dim = ORDERS[p][phase]
            k = pos[dim]
            right, left = neighbour(dim, 1), neighbour(dim, 3)
            far = (k + 2) % 4
            if phase == 0:
                piece(p, phase, far, None, 4, right).wait_recv()
            else:
                piece(p, phase, far, 0, 4, right).wait_recv()
                piece(p, phase, far, 1, 5, left).wait_recv()
            if phase == 2:
                go(to_sibling(p, region(p, 2, far, None), 3))
    for p in range(3):
        dim = ORDERS[p][2]
        k = pos[dim]
        for slot, at in enumerate((k, (k + 3) % 4, (k + 1) % 4, (k + 2) % 4)):
            done = ORDERS[p][:2]
            zhi, zlo = (ALL, ALL) if "z" in done else (at // 2, at % 2)
            xs = ALL if "x" in done else at
            ys = ALL if "y" in done else at
            ref = gs[p].at[zhi, xs, zlo, ys, 1 - core]
            to_sibling(p, ref, slot).wait_recv()
    for copy in sent:
        copy.wait_send()

    per = 32 // NR

    def a2a(r, j_to, src_h, h):
        cs = pl.ds(r * per, per)
        return pltpu.make_async_remote_copy(
            src_ref=dressed.at[h, cs], dst_ref=recv.at[src_h, cs],
            send_sem=a2a_send.at[r, h], recv_sem=a2a_recv.at[r, src_h],
            device_id=(occ, h * 2 + core), device_id_type=MESH,
        )

    def a2a_own(r):
        cs = pl.ds(r * per, per)
        return pltpu.make_async_copy(
            dressed.at[my_h, cs], recv.at[my_h, cs], a2a_recv.at[r, my_h]
        )

    def peer(j):
        return (zl + j // 4) % 2 * 4 + (y + j) % 4

    def dress(step, carry):
        r, j = step // 8, 7 - step % 8
        h = peer(j)
        block, high, low, bound = (table[i, h] for i in range(4))
        weights = jnp.concatenate(
            [g[high, low].reshape(BLK, w) for g, w in zip(gs, WIDTHS)], axis=1
        )
        cs = pl.ds(r * per, per)
        rows = jnp.concatenate([amp[i, cs].reshape(per * 32, BLK) for i in range(8)], axis=1)
        value = lax.dot_general(
            rows, weights, (((1,), (1,)), ((), ())), preferred_element_type=F32
        )
        value += amp[block, cs].reshape(per * 32, BLK).astype(F32)
        value = jnp.where(lane < bound, value, 0.0).astype(BF16)
        dressed[h, cs] = value.reshape(per, 32, BLK)

        @pl.when(j != 0)
        def _():
            a2a(r, j, my_h, h).start()

        @pl.when(j == 0)
        def _():
            a2a_own(r).start()

        return carry

    lax.fori_loop(0, NR * 8, dress, 0)

    slab_copy.wait_send()
    other = pl.ds(pl.multiple_of((1 - core) * 128, 128), 128)
    pltpu.make_async_remote_copy(
        src_ref=slab.at[:, :, other], dst_ref=slab.at[:, :, other],
        send_sem=fin_sem.at[0], recv_sem=fin_sem.at[1],
        device_id=sibling, device_id_type=MESH,
    ).wait_recv()
    total[...] = jnp.zeros_like(total)

    def ladder(r, carry):
        def arrived(j, inner):
            h = peer(j)
            a2a(r, j, h, h).wait_recv()
            return inner

        lax.fori_loop(1, 8, arrived, 0)
        a2a_own(r).wait()

        def one(c, inner):
            rows = recv[:, c].reshape(8 * 32, BLK)
            total[...] += jnp.dot(rows, slab[c], preferred_element_type=F32)
            return inner

        lax.fori_loop(r * per, (r + 1) * per, one, 0)
        return carry

    lax.fori_loop(0, NR, ladder, 0)

    live = lane < counts[my_h]
    result = jnp.where(live, total[...], 0.0).astype(BF16).reshape(8, 32, BLK)
    keep = jnp.where(core == 0, result[:, :, :128], result[:, :, 128:])
    give = jnp.where(core == 0, result[:, :, 128:], result[:, :, :128])
    mine[...] = give
    swap = pltpu.make_async_remote_copy(
        src_ref=mine, dst_ref=theirs, send_sem=fin_sem.at[2], recv_sem=fin_sem.at[3],
        device_id=sibling, device_id_type=MESH,
    )
    swap.start()
    out_ref[:, core] = keep

    def drain(step, carry):
        r, j = step // 7, 1 + step % 7
        a2a(r, j, my_h, peer(j)).wait_send()
        return carry

    lax.fori_loop(0, NR * 7, drain, 0)
    swap.wait()
    out_ref[:, 1 - core] = theirs[...]


def body(amplitudes, cycle_inter, ladder_slab, irrep_counts, slab_irrep):
    any_spec = pl.BlockSpec(memory_space=pl.ANY)
    smem = pl.BlockSpec(memory_space=pltpu.SMEM)
    dma = pltpu.SemaphoreType.DMA
    block = jnp.arange(8, dtype=jnp.int32) ^ slab_irrep[0]
    table = jnp.stack([block, block // 4, block % 4, irrep_counts[block]])
    out = pl.pallas_call(
        kernel,
        out_shape=jax.ShapeDtypeStruct((8, 2, 32, 128), BF16),
        in_specs=[any_spec, any_spec, any_spec, smem, smem],
        out_specs=pl.BlockSpec(memory_space=pltpu.VMEM),
        scratch_shapes=[
            pltpu.VMEM((32, 32, 2048), BF16),
            pltpu.VMEM((2, 1024, 128), F32),
            pltpu.VMEM((8, 32, 32, BLK), BF16),
        ]
        + [pltpu.VMEM((2, 4, 2, 4, 2, 16, w), BF16) for w in WIDTHS]
        + [
            pltpu.VMEM((8, 32, 32, BLK), BF16),
            pltpu.VMEM((8, 32, 32, BLK), BF16),
            pltpu.VMEM((32, BLK, BLK), BF16),
            pltpu.VMEM((BLK, BLK), F32),
            pltpu.VMEM((8, 32, 128), BF16),
            pltpu.VMEM((8, 32, 128), BF16),
            dma((5,)),
            dma((3, 3, 6)),
            dma((3, 3, 6)),
            dma((3, 4)),
            dma((3, 4)),
            dma((NR, 8)),
            dma((NR, 8)),
            dma((4,)),
        ],
        compiler_params=pltpu.CompilerParams(
            collective_id=0, has_side_effects=True, vmem_limit_bytes=56 * 1024 * 1024
        ),
        cost_estimate=pl.CostEstimate(
            flops=11 * 10**9, bytes_accessed=7 * 10**6, transcendentals=0
        ),
    )(amplitudes, cycle_inter.T, ladder_slab, irrep_counts, table)
    return out.reshape(512, 128)


def solution(mesh):
    placed = (
        P(("occ", "vir"), None, None),
        P(None, ("occ", "vir")),
        P(None, None, "vir"),
        P(),
        P(),
    )
    return jax.shard_map(
        body, mesh=mesh, in_specs=placed, out_specs=P("occ", "vir"), check_vma=False
    )
```

```python
import jax
import jax.numpy as jnp
from jax import lax
from jax.experimental import pallas as pl
from jax.experimental.pallas import tpu as pltpu
from jax.sharding import PartitionSpec as P

BLK = 256
WIDTHS = (768, 640, 640)
ORDERS = ("yzx", "zxy", "xyz")
NR = 4
MESH = pl.DeviceIdType.MESH
F32 = jnp.float32
BF16 = jnp.bfloat16
ALL = slice(None)


def device(x, y, z, core):
    return (z // 2 * 4 + x, z % 2 * 8 + y * 2 + core)


def kernel(
    amp_hbm, cyc_hbm, slab_hbm, counts, table, out_ref,
    raw, trans, amp, g0, g1, g2, dressed, recv, slab, total, result, near, beyond,
    local_sem, gather_send, gather_recv, sib_send, sib_recv, a2a_send, a2a_recv,
    slab_send, slab_recv, fin_send, fin_recv,
):
    occ, vir = lax.axis_index("occ"), lax.axis_index("vir")
    x, y, core = occ % 4, vir // 2 % 4, vir % 2
    zh, zl = occ // 4, vir // 8
    z = zh * 2 + zl
    gs = (g0, g1, g2)
    pos = {"x": x, "y": y, "z": z}
    sibling = device(x, y, z, 1 - core)
    z_inner = (z + 1 + 2 * zl) % 4
    z_outer = (z + 3 + 2 * zl) % 4
    z_of = (z, z_inner, z_outer)

    def neighbour(dim, step):
        at = dict(pos)
        at[dim] = (at[dim] + step) % 4
        return device(at["x"], at["y"], at["z"], core)

    load_amp = pltpu.make_async_copy(amp_hbm, raw, local_sem.at[0])
    load_amp.start()
    half = pl.ds(pl.multiple_of(core * 128, 128), 128)
    load_slab = pltpu.make_async_copy(slab_hbm, slab.at[0, :, :, half], local_sem.at[1])
    load_slab.start()
    offset = 0
    load_cyc = []
    for p in range(3):
        w = WIDTHS[p]
        load_cyc.append(
            pltpu.make_async_copy(
                cyc_hbm.at[:, pl.ds(offset, w)], gs[p].at[zh, x, zl, y, core], local_sem.at[2 + p]
            )
        )
        load_cyc[-1].start()
        offset += w

    barrier = pltpu.get_barrier_semaphore()
    greet = [sibling, neighbour("x", 1), neighbour("x", 3)]
    greet += [device(x, y, z_inner, core), device(x, y, z_outer, core)]
    for step in (1, 3):
        greet += [device(x, (y + step) % 4, zt, core) for zt in z_of]
        greet.append(device(x, (y + step) % 4, z, 1 - core))
    for step in (0, 1, 3):
        greet += [device(x, (y + step) % 4, (z + 2) % 4, c) for c in range(2)]
    for who in greet:
        pl.semaphore_signal(barrier, inc=1, device_id=who, device_id_type=MESH)
    pl.semaphore_wait(barrier, len(greet))

    def region(p, phase, k, part):
        done = ORDERS[p][:phase]
        dim = ORDERS[p][phase]
        at = {}
        for name in "xyz":
            at[name] = ALL if name in done else pos[name]
        at[dim] = k
        zhi, zlo = (ALL, ALL) if "z" in done else (at["z"] // 2, at["z"] % 2)
        xs, ys = at["x"], at["y"]
        if part is not None and phase > 0:
            if "z" in done:
                zhi = part
            elif "x" in done:
                xs = pl.ds(2 * part, 2)
            else:
                ys = pl.ds(2 * part, 2)
        return gs[p].at[zhi, xs, zlo, ys, core]

    def piece(p, phase, k, part, slot, who):
        ref = region(p, phase, k, part)
        return pltpu.make_async_remote_copy(
            src_ref=ref, dst_ref=ref,
            send_sem=gather_send.at[p, phase, slot], recv_sem=gather_recv.at[p, phase, slot],
            device_id=who, device_id_type=MESH,
        )

    def to_sibling(p, ref, slot):
        return pltpu.make_async_remote_copy(
            src_ref=ref, dst_ref=ref,
            send_sem=sib_send.at[p, slot], recv_sem=sib_recv.at[p, slot],
            device_id=sibling, device_id_type=MESH,
        )

    def sib_wait(p, ref_of, slot):
        ref = ref_of
        return pltpu.make_async_remote_copy(
            src_ref=ref, dst_ref=ref,
            send_sem=sib_send.at[p, slot], recv_sem=sib_recv.at[p, slot],
            device_id=sibling, device_id_type=MESH,
        )

    sent = []

    def go(copy):
        copy.start()
        sent.append(copy)

    lane = lax.broadcasted_iota(jnp.int32, (1, BLK), 1)

    def transpose_block(k):
        cols = pl.ds(pl.multiple_of(k * BLK, BLK), BLK)
        block = raw[:, :, cols].astype(F32)
        block = jnp.where((lane < counts[k])[None], block, 0.0)
        block = block.reshape(1024, BLK)
        trans[0] = block[:, :128]
        trans[1] = block[:, 128:]

        def one(c, carry):
            rows = pl.ds(c, 32, stride=32)
            pair = [trans[0, rows, :], trans[1, rows, :]]
            amp[k, c] = jnp.concatenate(pair, axis=1).astype(BF16)
            return carry

        lax.fori_loop(0, 32, one, 0, unroll=4)

    def transpose_blocks(first, last):
        def one(k, carry):
            transpose_block(k)
            return carry

        lax.fori_loop(first, last, one, 0)

    def slab_piece(which, first, count, side, slot, who):
        lanes = pl.ds(pl.multiple_of(side * 128, 128), 128)
        src = slab.at[which[0], pl.ds(first, count), :, lanes]
        dst = slab.at[which[1], pl.ds(first, count), :, lanes]
        return pltpu.make_async_remote_copy(
            src_ref=src, dst_ref=dst, send_sem=slab_send.at[slot], recv_sem=slab_recv.at[slot],
            device_id=who, device_id_type=MESH,
        )

    load_slab.wait()
    quarter = [(x + i) % 4 * 8 for i in range(4)]
    x_right, x_left = neighbour("x", 1), neighbour("x", 3)

    for phase in range(3):
        for p in range(3):
            dim = ORDERS[p][phase]
            k = pos[dim]
            right, left = neighbour(dim, 1), neighbour(dim, 3)
            if phase == 0:
                load_cyc[p].wait()
                go(piece(p, phase, k, None, 0, right))
                go(piece(p, phase, k, None, 1, left))
            else:
                go(piece(p, phase, k, 0, 0, right))
                go(piece(p, phase, k, 1, 1, left))
                go(piece(p, phase, k, 1, 2, right))
                go(piece(p, phase, k, 0, 3, left))
        if phase == 0:
            go(slab_piece((0, 1), quarter[0], 8, core, 0, neighbour("y", 3)))
            go(slab_piece((0, 0), 0, 32, core, 1, sibling))
            load_amp.wait()
            transpose_blocks(0, 1)
        if phase == 1:
            transpose_blocks(1, 3)
        if phase == 2:
            for p in range(3):
                dim = ORDERS[p][2]
                go(to_sibling(p, region(p, 2, pos[dim], None), 0))
            transpose_blocks(3, 8)
        for p in range(3):
            dim = ORDERS[p][phase]
            k = pos[dim]
            right, left = neighbour(dim, 1), neighbour(dim, 3)
            before, after = (k + 3) % 4, (k + 1) % 4
            if phase == 0:
                piece(p, phase, before, None, 0, right).wait_recv()
                piece(p, phase, after, None, 1, left).wait_recv()
                if p == 1:
                    go(piece(p, phase, after, None, 4, left))
                else:
                    go(piece(p, phase, before, None, 4, right))
            else:
                piece(p, phase, before, 0, 0, right).wait_recv()
                go(piece(p, phase, before, 0, 4, right))
                piece(p, phase, after, 1, 1, left).wait_recv()
                go(piece(p, phase, after, 1, 5, left))
        for p in range(3):
            dim = ORDERS[p][phase]
            k = pos[dim]
            right, left = neighbour(dim, 1), neighbour(dim, 3)
            before, after, far = (k + 3) % 4, (k + 1) % 4, (k + 2) % 4
            if phase > 0:
                piece(p, phase, before, 1, 2, right).wait_recv()
                piece(p, phase, after, 0, 3, left).wait_recv()
            if phase == 2:
                go(to_sibling(p, region(p, 2, before, None), 1))
                go(to_sibling(p, region(p, 2, after, None), 2))
        for p in range(3):
            dim = ORDERS[p][phase]
            k = pos[dim]
            right, left = neighbour(dim, 1), neighbour(dim, 3)
            far = (k + 2) % 4
            if phase == 0:
                piece(p, phase, far, None, 4, right).wait_recv()
            else:
                piece(p, phase, far, 0, 4, right).wait_recv()
                piece(p, phase, far, 1, 5, left).wait_recv()
            if phase == 2:
                go(to_sibling(p, region(p, 2, far, None), 3))
    for p in range(3):
        dim = ORDERS[p][2]
        k = pos[dim]
        for slot, at in enumerate((k, (k + 3) % 4, (k + 1) % 4, (k + 2) % 4)):
            done = ORDERS[p][:2]
            zhi, zlo = (ALL, ALL) if "z" in done else (at // 2, at % 2)
            xs = ALL if "x" in done else at
            ys = ALL if "y" in done else at
            ref = gs[p].at[zhi, xs, zlo, ys, 1 - core]
            to_sibling(p, ref, slot).wait_recv()

    slab_piece((0, 1), quarter[0], 8, core, 0, x_left).wait_recv()
    go(slab_piece((1, 1), quarter[0], 8, core, 2, x_right))
    go(slab_piece((1, 1), quarter[0], 8, core, 3, x_left))
    go(slab_piece((1, 1), quarter[0], 8, core, 6, sibling))

    per = 32 // NR
    spots = ((0, 0), (1, 0), (1, 1), (0, 1))
    y_of = (y, y, (y + 1) % 4, (y + 3) % 4)

    def message(r, dy, zt):
        cs = pl.ds(r * per, per)
        src = dressed.at[int(zt > 0), dy, cs]
        dst = recv.at[spots[dy][0], spots[dy][1], cs]
        if zt == 0:
            dst = recv.at[spots[dy][0], spots[dy][1], cs, pl.ds(0, 32)]
        else:
            src = dressed.at[1, dy, cs, pl.ds(16 * zt - 16, 16)]
            dst = recv.at[spots[dy][0], spots[dy][1], cs, pl.ds(16 + 16 * zt, 16)]
        return pltpu.make_async_remote_copy(
            src_ref=src, dst_ref=dst,
            send_sem=a2a_send.at[r, dy, zt], recv_sem=a2a_recv.at[r, dy, zt],
            device_id=device(x, y_of[dy], z_of[zt], core), device_id_type=MESH,
        )

    def kinds(dys):
        return [(dy, zt) for dy in dys for zt in range(3) if dy > 1 or zt > 0]

    def dress(r, carry):
        cs = pl.ds(r * per, per)
        for dys in ((2, 3), (0, 1)):
            blocks = [(dz, dy) for dy in dys for dz in range(2)]
            tables = []
            for dz, dy in blocks:
                h = (zl + dz) % 2 * 4 + (y + dy) % 4
                tables.append([table[i, h] for i in range(4)])
            weights = jnp.concatenate(
                [
                    jnp.concatenate(
                        [g[t[1], t[2]].reshape(BLK, w) for g, w in zip(gs, WIDTHS)], axis=1
                    )
                    for t in tables
                ],
                axis=0,
            )
            rows = jnp.concatenate([amp[i, cs].reshape(per * 32, BLK) for i in range(8)], axis=1)
            values = lax.dot_general(
                rows, weights, (((1,), (1,)), ((), ())), preferred_element_type=F32
            )
            for i, (dz, dy) in enumerate(blocks):
                value = values[:, i * BLK : (i + 1) * BLK]
                value += amp[tables[i][0], cs].reshape(per * 32, BLK).astype(F32)
                value = jnp.where(lane < tables[i][3], value, 0.0).astype(BF16)
                value = value.reshape(per, 32, BLK)
                if dz == 0 and dy < 2:
                    recv[spots[dy][0], spots[dy][1], cs, 0:32] = value
                else:
                    dressed[dz, dy, cs] = value
            for dy, zt in kinds(dys):
                message(r, dy, zt).start()

        @pl.when(r == 2)
        def _():
            slab_piece((1, 1), quarter[3], 8, core, 2, x_right).wait_recv()
            slab_piece((1, 1), quarter[3], 4, core, 4, x_right).start()
            slab_piece((1, 1), quarter[1], 8, core, 3, x_left).wait_recv()
            slab_piece((1, 1), quarter[1] + 4, 4, core, 5, x_left).start()
            slab_piece((1, 1), quarter[3], 8, core, 7, sibling).start()
            slab_piece((1, 1), quarter[1], 8, core, 8, sibling).start()

        return carry

    lax.fori_loop(0, NR, dress, 0)
    sent.append(slab_piece((1, 1), quarter[3], 4, core, 4, x_right))
    sent.append(slab_piece((1, 1), quarter[1] + 4, 4, core, 5, x_left))
    sent.append(slab_piece((1, 1), quarter[3], 8, core, 7, sibling))
    sent.append(slab_piece((1, 1), quarter[1], 8, core, 8, sibling))

    slab_piece((0, 0), 0, 32, 1 - core, 1, sibling).wait_recv()
    total[...] = jnp.zeros_like(total)

    def ladder(r, half_of):
        for dy in range(4):
            if spots[dy][0] == half_of:
                for kind in kinds((dy,)):
                    message(r, *kind).wait_recv()
        cs = pl.ds(r * per, per)
        rows = jnp.concatenate(
            [recv[half_of, :, r * per + c].reshape(128, BLK) for c in range(per)], axis=1
        )
        weights = slab[half_of, cs].reshape(per * BLK, BLK)
        total[half_of] += jnp.dot(rows, weights, preferred_element_type=F32)

    def ladder_first(r, carry):
        ladder(r, 0)
        return carry

    def ladder_second(r, carry):
        ladder(r, 1)
        return carry

    lax.fori_loop(0, NR - 1, ladder_first, 0)
    slab_piece((1, 1), quarter[2], 4, core, 4, x_right).wait_recv()
    slab_piece((1, 1), quarter[2] + 4, 4, core, 5, x_left).wait_recv()
    go(slab_piece((1, 1), quarter[2], 8, core, 9, sibling))
    for slot, q in ((6, 0), (7, 3), (8, 1), (9, 2)):
        slab_piece((1, 1), quarter[q], 8, 1 - core, slot, sibling).wait_recv()
    lax.fori_loop(0, NR - 1, ladder_second, 0)
    ladder(NR - 1, 0)
    ladder(NR - 1, 1)

    def home(which, place, side):
        at = device(x, (y + which) % 4, (z + 2 * place) % 4, side)
        land = (near, beyond)[place].at[which, core]
        rows = (pl.ds(0, 48), pl.ds(48, 16))[place]
        return pltpu.make_async_remote_copy(
            src_ref=result.at[which, side, :, rows], dst_ref=land,
            send_sem=fin_send.at[which, place, side], recv_sem=fin_recv.at[which, place, core],
            device_id=at, device_id_type=MESH,
        )

    for which in (1, 0):
        h = zl * 4 + (y + which) % 4
        value = jnp.where(lane < counts[h], total[which], 0.0).astype(BF16).reshape(2, 64, BLK)
        for side in range(2):
            result[which, side] = value[:, :, side * 128 : (side + 1) * 128]
        for place in (1, 0):
            for side in range(2):
                if which == 0 and place == 0:
                    @pl.when(core != side)
                    def _():
                        home(0, 0, side).start()
                else:
                    home(which, place, side).start()
    near[0, core] = result[0, core, :, 0:48]

    for copy in sent:
        copy.wait_send()

    def drain(r, carry):
        for dy, zt in kinds(range(4)):
            message(r, dy, zt).wait_send()
        return carry

    lax.fori_loop(0, NR, drain, 0)

    def arrival(which, place, side):
        land = (near, beyond)[place].at[which, side]
        rows = (pl.ds(0, 48), pl.ds(48, 16))[place]
        return pltpu.make_async_remote_copy(
            src_ref=result.at[which, side, :, rows], dst_ref=land,
            send_sem=fin_send.at[which, place, side], recv_sem=fin_recv.at[which, place, side],
            device_id=sibling, device_id_type=MESH,
        )

    for which in range(2):
        for place in range(2):
            for side in range(2):
                if which == 0 and place == 0:
                    @pl.when(core != side)
                    def _():
                        arrival(0, 0, side).wait()
                else:
                    arrival(which, place, side).wait()
    for which in range(2):
        for other in range(2):
            source = (y + ((0, 1), (3, 2))[which][other]) % 4
            for side in range(2):
                out_ref[zl, source, side] = near[which, side, other, 0:32]
                out_ref[1 - zl, source, side, 0:16] = near[which, side, other, 32:48]
                out_ref[1 - zl, source, side, 16:32] = beyond[which, side, other]


def body(amplitudes, cycle_inter, ladder_slab, irrep_counts, slab_irrep):
    any_spec = pl.BlockSpec(memory_space=pl.ANY)
    smem = pl.BlockSpec(memory_space=pltpu.SMEM)
    dma = pltpu.SemaphoreType.DMA
    block = jnp.arange(8, dtype=jnp.int32) ^ slab_irrep[0]
    table = jnp.stack([block, block // 4, block % 4, irrep_counts[block]])
    out = pl.pallas_call(
        kernel,
        out_shape=jax.ShapeDtypeStruct((2, 4, 2, 32, 128), BF16),
        in_specs=[any_spec, any_spec, any_spec, smem, smem],
        out_specs=pl.BlockSpec(memory_space=pltpu.VMEM),
        scratch_shapes=[
            pltpu.VMEM((32, 32, 2048), BF16),
            pltpu.VMEM((2, 1024, 128), F32),
            pltpu.VMEM((8, 32, 32, BLK), BF16),
        ]
        + [pltpu.VMEM((2, 4, 2, 4, 2, 16, w), BF16) for w in WIDTHS]
        + [
            pltpu.VMEM((2, 4, 32, 32, BLK), BF16),
            pltpu.VMEM((2, 2, 32, 64, BLK), BF16),
            pltpu.VMEM((2, 32, BLK, BLK), BF16),
            pltpu.VMEM((2, 128, BLK), F32),
            pltpu.VMEM((2, 2, 2, 64, 128), BF16),
            pltpu.VMEM((2, 2, 2, 48, 128), BF16),
            pltpu.VMEM((2, 2, 2, 16, 128), BF16),
            dma((5,)),
            dma((3, 3, 6)),
            dma((3, 3, 6)),
            dma((3, 4)),
            dma((3, 4)),
            dma((NR, 4, 3)),
            dma((NR, 4, 3)),
            dma((10,)),
            dma((10,)),
            dma((2, 2, 2)),
            dma((2, 2, 2)),
        ],
        compiler_params=pltpu.CompilerParams(
            collective_id=0, has_side_effects=True, vmem_limit_bytes=56 * 1024 * 1024
        ),
        cost_estimate=pl.CostEstimate(
            flops=11 * 10**9, bytes_accessed=7 * 10**6, transcendentals=0
        ),
    )(amplitudes, cycle_inter.T, ladder_slab, irrep_counts, table)
    return out.reshape(512, 128)


def solution(mesh):
    placed = (
        P(("occ", "vir"), None, None),
        P(None, ("occ", "vir")),
        P(None, None, "vir"),
        P(),
        P(),
    )
    return jax.shard_map(
        body, mesh=mesh, in_specs=placed, out_specs=P("occ", "vir"), check_vma=False
    )
```

```python
import jax
import jax.numpy as jnp
from jax import lax
from jax.experimental import pallas as pl
from jax.experimental.pallas import tpu as pltpu
from jax.sharding import PartitionSpec as P

BLK = 256
WIDTHS = (896, 256, 896)
ORDERS = ("yzx", "zxy", "xyz")
NR = 4
MESH = pl.DeviceIdType.MESH
F32 = jnp.float32
BF16 = jnp.bfloat16
ALL = slice(None)


def device(x, y, z, core):
    return (z // 2 * 4 + x, z % 2 * 8 + y * 2 + core)


def kernel(
    amp_hbm, cyc_hbm, slab_hbm, counts, table, out_ref,
    raw, trans, amp, g0, g1, g2, dressed, recv, slab, total, result, near, beyond,
    local_sem, gather_send, gather_recv, sib_send, sib_recv, a2a_send, a2a_recv,
    slab_send, slab_recv, fin_send, fin_recv,
):
    occ, vir = lax.axis_index("occ"), lax.axis_index("vir")
    x, y, core = occ % 4, vir // 2 % 4, vir % 2
    zh, zl = occ // 4, vir // 8
    z = zh * 2 + zl
    gs = (g0, g1, g2)
    pos = {"x": x, "y": y, "z": z}
    sibling = device(x, y, z, 1 - core)
    z_inner = (z + 1 + 2 * zl) % 4
    z_outer = (z + 3 + 2 * zl) % 4
    z_of = (z, z_inner, z_outer)

    def neighbour(dim, step):
        at = dict(pos)
        at[dim] = (at[dim] + step) % 4
        return device(at["x"], at["y"], at["z"], core)

    load_amp = pltpu.make_async_copy(amp_hbm, raw, local_sem.at[0])
    load_amp.start()
    half = pl.ds(pl.multiple_of(core * 128, 128), 128)
    load_slab = pltpu.make_async_copy(slab_hbm, slab.at[0, :, :, half], local_sem.at[1])
    load_slab.start()
    offset = 0
    load_cyc = []
    for p in range(3):
        w = WIDTHS[p]
        load_cyc.append(
            pltpu.make_async_copy(
                cyc_hbm.at[:, pl.ds(offset, w)], gs[p].at[zh, x, zl, y, core], local_sem.at[2 + p]
            )
        )
        load_cyc[-1].start()
        offset += w

    barrier = pltpu.get_barrier_semaphore()
    greet = [sibling] + [neighbour(dim, step) for dim in "xyz" for step in (1, 3, 2)]
    for who in greet:
        pl.semaphore_signal(barrier, inc=1, device_id=who, device_id_type=MESH)
    pl.semaphore_wait(barrier, len(greet))

    def region(p, second, third, part, side):
        d1, d2, d3 = ORDERS[p]
        at = {d1: ALL if part is None else pl.ds(2 * part, 2), d2: second, d3: third}
        zhi, zlo = at["z"] // 2 if at["z"] is not ALL and d1 != "z" else ALL, ALL
        if d1 == "z":
            zhi = ALL if part is None else part
        elif at["z"] is not ALL:
            zlo = at["z"] % 2
        return gs[p].at[zhi, at["x"], zlo, at["y"], side]

    def pass_on(p, second, third, part, slot, who):
        ref = region(p, second, third, part, core)
        return pltpu.make_async_remote_copy(
            src_ref=ref, dst_ref=ref,
            send_sem=gather_send.at[p, slot], recv_sem=gather_recv.at[p, slot],
            device_id=who, device_id_type=MESH,
        )

    def to_sibling(p, second, third, slot, side):
        ref = region(p, second, third, None, side)
        return pltpu.make_async_remote_copy(
            src_ref=ref, dst_ref=ref,
            send_sem=sib_send.at[p, slot], recv_sem=sib_recv.at[p, slot],
            device_id=sibling, device_id_type=MESH,
        )

    sent = []

    def go(copy):
        copy.start()
        sent.append(copy)

    lane = lax.broadcasted_iota(jnp.int32, (1, BLK), 1)

    def transpose_block(k):
        cols = pl.ds(pl.multiple_of(k * BLK, BLK), BLK)
        block = raw[:, :, cols].astype(F32)
        block = jnp.where((lane < counts[k])[None], block, 0.0)
        block = block.reshape(1024, BLK)
        trans[0] = block[:, :128]
        trans[1] = block[:, 128:]

        def one(c, carry):
            rows = pl.ds(c, 32, stride=32)
            pair = [trans[0, rows, :], trans[1, rows, :]]
            amp[k, c] = jnp.concatenate(pair, axis=1).astype(BF16)
            return carry

        lax.fori_loop(0, 32, one, 0, unroll=4)

    def transpose_blocks(first, last):
        def one(k, carry):
            transpose_block(k)
            return carry

        lax.fori_loop(first, last, one, 0)

    def slab_piece(which, first, count, side, slot, who):
        lanes = pl.ds(pl.multiple_of(side * 128, 128), 128)
        src = slab.at[which[0], pl.ds(first, count), :, lanes]
        dst = slab.at[which[1], pl.ds(first, count), :, lanes]
        return pltpu.make_async_remote_copy(
            src_ref=src, dst_ref=dst, send_sem=slab_send.at[slot], recv_sem=slab_recv.at[slot],
            device_id=who, device_id_type=MESH,
        )

    quarter = [(x + i) % 4 * 8 for i in range(4)]
    x_right, x_left = neighbour("x", 1), neighbour("x", 3)

    def first(p, step, source):
        d1 = ORDERS[p][0]
        at = dict(pos)
        at[d1] = (at[d1] + source) % 4
        ref = gs[p].at[at["z"] // 2, at["x"], at["z"] % 2, at["y"], core]
        return pltpu.make_async_remote_copy(
            src_ref=ref, dst_ref=ref,
            send_sem=gather_send.at[p, step - 1], recv_sem=gather_recv.at[p, step - 1],
            device_id=neighbour(d1, step), device_id_type=MESH,
        )

    offsets = (0, 3, 1, 2)
    seconds = [[(pos[ORDERS[p][1]] + i) % 4 for i in offsets] for p in range(3)]
    thirds = [[(pos[ORDERS[p][2]] + i) % 4 for i in offsets] for p in range(3)]
    ends = [
        [(neighbour(ORDERS[p][i], 1), neighbour(ORDERS[p][i], 3)) for i in range(3)]
        for p in range(3)
    ]

    def along_second(p, i, part, slot):
        return pass_on(p, seconds[p][i], thirds[p][0], part, 3 + slot, ends[p][1][slot % 2])

    def along_third(p, sub, i, part, slot):
        return pass_on(p, seconds[p][sub], thirds[p][i], part, 7 + 4 * sub + slot, ends[p][2][slot % 2])

    def spread(p, sub):
        go(along_third(p, sub, 0, None, 0))
        go(along_third(p, sub, 0, None, 1))

    def forward_third(p, sub):
        along_third(p, sub, 1, None, 0).wait_recv()
        go(along_third(p, sub, 1, 0, 2))
        along_third(p, sub, 2, None, 1).wait_recv()
        go(along_third(p, sub, 2, 1, 3))

    def slab_fetch(first, slot):
        lanes = pl.ds(pl.multiple_of(core * 128, 128), 128)
        return pltpu.make_async_remote_copy(
            src_ref=slab_hbm.at[pl.ds(first, 8)], dst_ref=slab.at[1, pl.ds(first, 8), :, lanes],
            send_sem=slab_send.at[slot], recv_sem=slab_recv.at[slot],
            device_id=neighbour("y", 3), device_id_type=MESH,
        )

    for p in range(3):
        load_cyc[p].wait()
        for step in (1, 3, 2):
            go(first(p, step, 0))
    load_amp.wait()
    transpose_blocks(0, 1)
    for p in range(3):
        for step in (1, 3, 2):
            first(p, step, 4 - step).wait_recv()
        go(along_second(p, 0, None, 0))
        go(along_second(p, 0, None, 1))
        spread(p, 0)
    load_slab.wait()
    go(slab_piece((0, 0), 0, 32, core, 1, sibling))
    transpose_blocks(1, 3)
    for p in range(3):
        along_second(p, 1, None, 0).wait_recv()
        go(along_second(p, 1, 0, 2))
        spread(p, 1)
        along_second(p, 2, None, 1).wait_recv()
        go(along_second(p, 2, 1, 3))
        spread(p, 2)
    for p in range(3):
        forward_third(p, 0)
    for p in range(3):
        along_second(p, 3, 0, 2).wait_recv()
        along_second(p, 3, 1, 3).wait_recv()
        spread(p, 3)
        go(to_sibling(p, ALL, thirds[p][0], 0, core))
    go(slab_fetch(quarter[0], 0))
    transpose_blocks(3, 8)
    for sub in (1, 2, 3):
        for p in range(3):
            forward_third(p, sub)
    for p in range(3):
        go(to_sibling(p, ALL, thirds[p][1], 1, core))
        go(to_sibling(p, ALL, thirds[p][2], 2, core))
    for sub in range(4):
        for p in range(3):
            along_third(p, sub, 3, 0, 2).wait_recv()
            along_third(p, sub, 3, 1, 3).wait_recv()
            go(to_sibling(p, seconds[p][sub], thirds[p][3], 3 + sub, core))
    for p in range(3):
        for i in range(3):
            to_sibling(p, ALL, thirds[p][i], i, 1 - core).wait_recv()
        for sub in range(4):
            to_sibling(p, seconds[p][sub], thirds[p][3], 3 + sub, 1 - core).wait_recv()
    slab_piece((0, 1), quarter[0], 8, core, 0, x_left).wait_recv()
    go(slab_piece((1, 1), quarter[0], 8, core, 2, x_right))
    go(slab_piece((1, 1), quarter[0], 8, core, 3, x_left))
    go(slab_piece((1, 1), quarter[0], 8, core, 6, sibling))

    per = 32 // NR
    spots = ((0, 0), (1, 0), (1, 1), (0, 1))
    y_of = (y, y, (y + 1) % 4, (y + 3) % 4)

    def message(r, dy, zt):
        cs = pl.ds(r * per, per)
        src = dressed.at[int(zt > 0), dy, cs]
        dst = recv.at[spots[dy][0], spots[dy][1], cs]
        if zt == 0:
            dst = recv.at[spots[dy][0], spots[dy][1], cs, pl.ds(0, 32)]
        else:
            src = dressed.at[1, dy, cs, pl.ds(16 * zt - 16, 16)]
            dst = recv.at[spots[dy][0], spots[dy][1], cs, pl.ds(16 + 16 * zt, 16)]
        return pltpu.make_async_remote_copy(
            src_ref=src, dst_ref=dst,
            send_sem=a2a_send.at[r, dy, zt], recv_sem=a2a_recv.at[r, dy, zt],
            device_id=device(x, y_of[dy], z_of[zt], core), device_id_type=MESH,
        )

    def kinds(dys):
        return [(dy, zt) for dy in dys for zt in range(3) if dy > 1 or zt > 0]

    def dress(r, carry):
        cs = pl.ds(r * per, per)
        for dys in ((2, 3), (0, 1)):
            blocks = [(dz, dy) for dy in dys for dz in range(2)]
            tables = []
            for dz, dy in blocks:
                h = (zl + dz) % 2 * 4 + (y + dy) % 4
                tables.append([table[i, h] for i in range(3)])
            weights = jnp.concatenate(
                [
                    jnp.concatenate(
                        [g[t[1], t[2]].reshape(BLK, w) for g, w in zip(gs, WIDTHS)], axis=1
                    )
                    for t in tables
                ],
                axis=0,
            )
            rows = jnp.concatenate([amp[i, cs].reshape(per * 32, BLK) for i in range(8)], axis=1)
            values = lax.dot_general(
                rows, weights, (((1,), (1,)), ((), ())), preferred_element_type=F32
            )
            for i, (dz, dy) in enumerate(blocks):
                value = values[:, i * BLK : (i + 1) * BLK]
                value += amp[tables[i][0], cs].reshape(per * 32, BLK).astype(F32)
                value = jnp.where(lane < counts[tables[i][0]], value, 0.0).astype(BF16)
                value = value.reshape(per, 32, BLK)
                if dz == 0 and dy < 2:
                    recv[spots[dy][0], spots[dy][1], cs, 0:32] = value
                else:
                    dressed[dz, dy, cs] = value
            for dy, zt in kinds(dys):
                message(r, dy, zt).start()

        @pl.when(r == 2)
        def _():
            slab_piece((1, 1), quarter[3], 8, core, 2, x_right).wait_recv()
            slab_piece((1, 1), quarter[3], 4, core, 4, x_right).start()
            slab_piece((1, 1), quarter[1], 8, core, 3, x_left).wait_recv()
            slab_piece((1, 1), quarter[1] + 4, 4, core, 5, x_left).start()
            slab_piece((1, 1), quarter[3], 8, core, 7, sibling).start()
            slab_piece((1, 1), quarter[1], 8, core, 8, sibling).start()

        return carry

    lax.fori_loop(0, NR, dress, 0)
    sent.append(slab_piece((1, 1), quarter[3], 4, core, 4, x_right))
    sent.append(slab_piece((1, 1), quarter[1] + 4, 4, core, 5, x_left))
    sent.append(slab_piece((1, 1), quarter[3], 8, core, 7, sibling))
    sent.append(slab_piece((1, 1), quarter[1], 8, core, 8, sibling))

    slab_piece((0, 0), 0, 32, 1 - core, 1, sibling).wait_recv()
    total[...] = jnp.zeros_like(total)

    def ladder(r, half_of):
        for dy in range(4):
            if spots[dy][0] == half_of:
                for kind in kinds((dy,)):
                    message(r, *kind).wait_recv()
        cs = pl.ds(r * per, per)
        rows = jnp.concatenate(
            [recv[half_of, :, r * per + c].reshape(128, BLK) for c in range(per)], axis=1
        )
        weights = slab[half_of, cs].reshape(per * BLK, BLK)
        total[half_of] += jnp.dot(rows, weights, preferred_element_type=F32)

    def ladder_first(r, carry):
        ladder(r, 0)
        return carry

    def ladder_second(r, carry):
        ladder(r, 1)
        return carry

    lax.fori_loop(0, NR - 1, ladder_first, 0)
    slab_piece((1, 1), quarter[2], 4, core, 4, x_right).wait_recv()
    slab_piece((1, 1), quarter[2] + 4, 4, core, 5, x_left).wait_recv()
    go(slab_piece((1, 1), quarter[2], 8, core, 9, sibling))
    for slot, q in ((6, 0), (7, 3), (8, 1), (9, 2)):
        slab_piece((1, 1), quarter[q], 8, 1 - core, slot, sibling).wait_recv()
    lax.fori_loop(0, NR - 1, ladder_second, 0)
    ladder(NR - 1, 0)
    ladder(NR - 1, 1)

    def home(which, place, side):
        at = device(x, (y + which) % 4, (z + 2 * place) % 4, side)
        land = (near, beyond)[place].at[which, core]
        rows = (pl.ds(0, 48), pl.ds(48, 16))[place]
        return pltpu.make_async_remote_copy(
            src_ref=result.at[which, side, :, rows], dst_ref=land,
            send_sem=fin_send.at[which, place, side], recv_sem=fin_recv.at[which, place, core],
            device_id=at, device_id_type=MESH,
        )

    for which in (1, 0):
        h = zl * 4 + (y + which) % 4
        value = jnp.where(lane < counts[h], total[which], 0.0).astype(BF16).reshape(2, 64, BLK)
        for side in range(2):
            result[which, side] = value[:, :, side * 128 : (side + 1) * 128]
        for place in (1, 0):
            for side in range(2):
                if which == 0 and place == 0:
                    @pl.when(core != side)
                    def _():
                        home(0, 0, side).start()
                else:
                    home(which, place, side).start()
    near[0, core] = result[0, core, :, 0:48]

    for copy in sent:
        copy.wait_send()

    def drain(r, carry):
        for dy, zt in kinds(range(4)):
            message(r, dy, zt).wait_send()
        return carry

    lax.fori_loop(0, NR, drain, 0)

    def arrival(which, place, side):
        land = (near, beyond)[place].at[which, side]
        rows = (pl.ds(0, 48), pl.ds(48, 16))[place]
        return pltpu.make_async_remote_copy(
            src_ref=result.at[which, side, :, rows], dst_ref=land,
            send_sem=fin_send.at[which, place, side], recv_sem=fin_recv.at[which, place, side],
            device_id=sibling, device_id_type=MESH,
        )

    for which in range(2):
        for place in range(2):
            for side in range(2):
                if which == 0 and place == 0:
                    @pl.when(core != side)
                    def _():
                        arrival(0, 0, side).wait()
                else:
                    arrival(which, place, side).wait()
    for which in range(2):
        for other in range(2):
            source = (y + ((0, 1), (3, 2))[which][other]) % 4
            for side in range(2):
                out_ref[zl, source, side] = near[which, side, other, 0:32]
                out_ref[1 - zl, source, side, 0:16] = near[which, side, other, 32:48]
                out_ref[1 - zl, source, side, 16:32] = beyond[which, side, other]


def body(amplitudes, cycle_inter, ladder_slab, irrep_counts, slab_irrep):
    any_spec = pl.BlockSpec(memory_space=pl.ANY)
    smem = pl.BlockSpec(memory_space=pltpu.SMEM)
    dma = pltpu.SemaphoreType.DMA
    block = lax.broadcasted_iota(jnp.int32, (3, 8), 1) ^ slab_irrep[0]
    row = lax.broadcasted_iota(jnp.int32, (3, 8), 0)
    table = jnp.where(row == 0, block, jnp.where(row == 1, block >> 2, block & 3))
    out = pl.pallas_call(
        kernel,
        out_shape=jax.ShapeDtypeStruct((2, 4, 2, 32, 128), BF16),
        in_specs=[any_spec, any_spec, any_spec, smem, smem],
        out_specs=pl.BlockSpec(memory_space=pltpu.VMEM),
        scratch_shapes=[
            pltpu.VMEM((32, 32, 2048), BF16),
            pltpu.VMEM((2, 1024, 128), F32),
            pltpu.VMEM((8, 32, 32, BLK), BF16),
        ]
        + [pltpu.VMEM((2, 4, 2, 4, 2, 16, w), BF16) for w in WIDTHS]
        + [
            pltpu.VMEM((2, 4, 32, 32, BLK), BF16),
            pltpu.VMEM((2, 2, 32, 64, BLK), BF16),
            pltpu.VMEM((2, 32, BLK, BLK), BF16),
            pltpu.VMEM((2, 128, BLK), F32),
            pltpu.VMEM((2, 2, 2, 64, 128), BF16),
            pltpu.VMEM((2, 2, 2, 48, 128), BF16),
            pltpu.VMEM((2, 2, 2, 16, 128), BF16),
            dma((5,)),
            dma((3, 23)),
            dma((3, 23)),
            dma((3, 7)),
            dma((3, 7)),
            dma((NR, 4, 3)),
            dma((NR, 4, 3)),
            dma((10,)),
            dma((10,)),
            dma((2, 2, 2)),
            dma((2, 2, 2)),
        ],
        compiler_params=pltpu.CompilerParams(
            collective_id=0, has_side_effects=True, vmem_limit_bytes=56 * 1024 * 1024
        ),
        cost_estimate=pl.CostEstimate(
            flops=11 * 10**9, bytes_accessed=7 * 10**6, transcendentals=0
        ),
    )(amplitudes, cycle_inter.T, ladder_slab, irrep_counts, table)
    return out.reshape(512, 128)


def solution(mesh):
    placed = (
        P(("occ", "vir"), None, None),
        P(None, ("occ", "vir")),
        P(None, None, "vir"),
        P(),
        P(),
    )
    return jax.shard_map(
        body, mesh=mesh, in_specs=placed, out_specs=P("occ", "vir"), check_vma=False
    )
```

```python
import jax
import jax.numpy as jnp
from jax import lax
from jax.experimental import pallas as pl
from jax.experimental.pallas import tpu as pltpu
from jax.sharding import PartitionSpec as P

BLK = 256
WIDTHS = (768, 512, 768)
ORDERS = ("yzx", "zxy", "xyz")
NR = 4
MESH = pl.DeviceIdType.MESH
F32 = jnp.float32
BF16 = jnp.bfloat16
ALL = slice(None)


def device(x, y, z, core):
    return (z // 2 * 4 + x, z % 2 * 8 + y * 2 + core)


def kernel(
    amp_hbm, cyc_hbm, slab_hbm, counts, table, out_ref,
    raw, trans, amp, g0, g1, g2, dressed, recv, slab, total, result, near, beyond,
    local_sem, gather_send, gather_recv, sib_send, sib_recv, a2a_send, a2a_recv,
    slab_send, slab_recv, fin_send, fin_recv,
):
    occ, vir = lax.axis_index("occ"), lax.axis_index("vir")
    x, y, core = occ % 4, vir // 2 % 4, vir % 2
    zh, zl = occ // 4, vir // 8
    z = zh * 2 + zl
    gs = (g0, g1, g2)
    pos = {"x": x, "y": y, "z": z}
    sibling = device(x, y, z, 1 - core)
    z_inner = (z + 1 + 2 * zl) % 4
    z_outer = (z + 3 + 2 * zl) % 4
    z_of = (z, z_inner, z_outer)

    def neighbour(dim, step):
        at = dict(pos)
        at[dim] = (at[dim] + step) % 4
        return device(at["x"], at["y"], at["z"], core)

    load_amp = pltpu.make_async_copy(amp_hbm, raw, local_sem.at[0])
    load_amp.start()
    half = pl.ds(pl.multiple_of(core * 128, 128), 128)
    load_slab = pltpu.make_async_copy(slab_hbm, slab.at[0, :, :, half], local_sem.at[1])
    load_slab.start()
    offset = 0
    load_cyc = []
    for p in range(3):
        w = WIDTHS[p]
        load_cyc.append(
            pltpu.make_async_copy(
                cyc_hbm.at[:, pl.ds(offset, w)], gs[p].at[zh, x, zl, y, core], local_sem.at[2 + p]
            )
        )
        load_cyc[-1].start()
        offset += w

    barrier = pltpu.get_barrier_semaphore()
    greet = [sibling] + [neighbour(dim, step) for dim in "xyz" for step in (1, 3, 2)]
    for who in greet:
        pl.semaphore_signal(barrier, inc=1, device_id=who, device_id_type=MESH)
    pl.semaphore_wait(barrier, len(greet))

    def region(p, second, third, part, side):
        d1, d2, d3 = ORDERS[p]
        at = {d1: ALL if part is None else pl.ds(2 * part, 2), d2: second, d3: third}
        zhi, zlo = at["z"] // 2 if at["z"] is not ALL and d1 != "z" else ALL, ALL
        if d1 == "z":
            zhi = ALL if part is None else part
        elif at["z"] is not ALL:
            zlo = at["z"] % 2
        return gs[p].at[zhi, at["x"], zlo, at["y"], side]

    def pass_on(p, second, third, part, slot, who):
        ref = region(p, second, third, part, core)
        return pltpu.make_async_remote_copy(
            src_ref=ref, dst_ref=ref,
            send_sem=gather_send.at[p, slot], recv_sem=gather_recv.at[p, slot],
            device_id=who, device_id_type=MESH,
        )

    def to_sibling(p, second, third, slot, side):
        ref = region(p, second, third, None, side)
        return pltpu.make_async_remote_copy(
            src_ref=ref, dst_ref=ref,
            send_sem=sib_send.at[p, slot], recv_sem=sib_recv.at[p, slot],
            device_id=sibling, device_id_type=MESH,
        )

    sent = []

    def go(copy):
        copy.start()
        sent.append(copy)

    lane = lax.broadcasted_iota(jnp.int32, (1, BLK), 1)

    def transpose_block(k):
        cols = pl.ds(pl.multiple_of(k * BLK, BLK), BLK)
        block = raw[:, :, cols].astype(F32)
        block = jnp.where((lane < counts[k])[None], block, 0.0)
        block = block.reshape(1024, BLK)
        trans[0] = block[:, :128]
        trans[1] = block[:, 128:]

        def one(c, carry):
            rows = pl.ds(c, 32, stride=32)
            pair = [trans[0, rows, :], trans[1, rows, :]]
            amp[k, c] = jnp.concatenate(pair, axis=1).astype(BF16)
            return carry

        lax.fori_loop(0, 32, one, 0, unroll=4)

    def transpose_blocks(first, last):
        def one(k, carry):
            transpose_block(k)
            return carry

        lax.fori_loop(first, last, one, 0)

    def slab_piece(which, first, count, side, slot, who):
        lanes = pl.ds(pl.multiple_of(side * 128, 128), 128)
        src = slab.at[which[0], pl.ds(first, count), :, lanes]
        dst = slab.at[which[1], pl.ds(first, count), :, lanes]
        return pltpu.make_async_remote_copy(
            src_ref=src, dst_ref=dst, send_sem=slab_send.at[slot], recv_sem=slab_recv.at[slot],
            device_id=who, device_id_type=MESH,
        )

    quarter = [(x + i) % 4 * 8 for i in range(4)]
    x_right, x_left = neighbour("x", 1), neighbour("x", 3)

    def first(p, step, source):
        d1 = ORDERS[p][0]
        at = dict(pos)
        at[d1] = (at[d1] + source) % 4
        ref = gs[p].at[at["z"] // 2, at["x"], at["z"] % 2, at["y"], core]
        return pltpu.make_async_remote_copy(
            src_ref=ref, dst_ref=ref,
            send_sem=gather_send.at[p, step - 1], recv_sem=gather_recv.at[p, step - 1],
            device_id=neighbour(d1, step), device_id_type=MESH,
        )

    offsets = (0, 3, 1, 2)
    seconds = [[(pos[ORDERS[p][1]] + i) % 4 for i in offsets] for p in range(3)]
    thirds = [[(pos[ORDERS[p][2]] + i) % 4 for i in offsets] for p in range(3)]
    steps = (1, 3, 2)

    def along_second(p, i, slot):
        who = neighbour(ORDERS[p][1], steps[slot])
        return pass_on(p, seconds[p][i], thirds[p][0], None, 3 + slot, who)

    def along_third(p, sub, i, slot):
        who = neighbour(ORDERS[p][2], steps[slot])
        return pass_on(p, seconds[p][sub], thirds[p][i], None, 6 + 3 * sub + slot, who)

    def spread(p, sub):
        for slot in range(3):
            go(along_third(p, sub, 0, slot))

    def slab_fetch(first, slot):
        lanes = pl.ds(pl.multiple_of(core * 128, 128), 128)
        return pltpu.make_async_remote_copy(
            src_ref=slab_hbm.at[pl.ds(first, 8)], dst_ref=slab.at[1, pl.ds(first, 8), :, lanes],
            send_sem=slab_send.at[slot], recv_sem=slab_recv.at[slot],
            device_id=neighbour("y", 3), device_id_type=MESH,
        )

    for p in range(3):
        load_cyc[p].wait()
        for step in steps:
            go(first(p, step, 0))
    load_amp.wait()
    transpose_blocks(0, 1)
    for p in range(3):
        for step in steps:
            first(p, step, 4 - step).wait_recv()
        for slot in range(3):
            go(along_second(p, 0, slot))
        spread(p, 0)
    load_slab.wait()
    go(slab_piece((0, 0), 0, 32, core, 1, sibling))
    transpose_blocks(1, 3)
    for slot in range(3):
        for p in range(3):
            along_second(p, slot + 1, slot).wait_recv()
            spread(p, slot + 1)
    go(slab_fetch(quarter[0], 0))
    transpose_blocks(3, 8)
    for sub in range(4):
        for p in range(3):
            for slot in range(3):
                along_third(p, sub, slot + 1, slot).wait_recv()
            go(to_sibling(p, seconds[p][sub], ALL, sub, core))
    for p in range(3):
        for sub in range(4):
            to_sibling(p, seconds[p][sub], ALL, sub, 1 - core).wait_recv()
    per = 32 // NR
    spots = ((0, 0), (1, 0), (1, 1), (0, 1))
    y_of = (y, y, (y + 1) % 4, (y + 3) % 4)

    def message(r, dy, zt):
        cs = pl.ds(r * per, per)
        src = dressed.at[int(zt > 0), dy, cs]
        dst = recv.at[spots[dy][0], spots[dy][1], cs]
        if zt == 0:
            dst = recv.at[spots[dy][0], spots[dy][1], cs, pl.ds(0, 32)]
        else:
            src = dressed.at[1, dy, cs, pl.ds(16 * zt - 16, 16)]
            dst = recv.at[spots[dy][0], spots[dy][1], cs, pl.ds(16 + 16 * zt, 16)]
        return pltpu.make_async_remote_copy(
            src_ref=src, dst_ref=dst,
            send_sem=a2a_send.at[r, dy, zt], recv_sem=a2a_recv.at[r, dy, zt],
            device_id=device(x, y_of[dy], z_of[zt], core), device_id_type=MESH,
        )

    def kinds(dys):
        return [(dy, zt) for dy in dys for zt in range(3) if dy > 1 or zt > 0]

    def dress(r, carry):
        cs = pl.ds(r * per, per)
        for dys in ((2, 3), (0, 1)):
            blocks = [(dz, dy) for dy in dys for dz in range(2)]
            tables = []
            for dz, dy in blocks:
                h = (zl + dz) % 2 * 4 + (y + dy) % 4
                tables.append([table[i, h] for i in range(3)])
            weights = jnp.concatenate(
                [
                    jnp.concatenate(
                        [g[t[1], t[2]].reshape(BLK, w) for g, w in zip(gs, WIDTHS)], axis=1
                    )
                    for t in tables
                ],
                axis=0,
            )
            rows = jnp.concatenate([amp[i, cs].reshape(per * 32, BLK) for i in range(8)], axis=1)
            values = lax.dot_general(
                rows, weights, (((1,), (1,)), ((), ())), preferred_element_type=F32
            )
            for i, (dz, dy) in enumerate(blocks):
                value = values[:, i * BLK : (i + 1) * BLK]
                value += amp[tables[i][0], cs].reshape(per * 32, BLK).astype(F32)
                value = jnp.where(lane < counts[tables[i][0]], value, 0.0).astype(BF16)
                value = value.reshape(per, 32, BLK)
                if dz == 0 and dy < 2:
                    recv[spots[dy][0], spots[dy][1], cs, 0:32] = value
                else:
                    dressed[dz, dy, cs] = value
            for dy, zt in kinds(dys):
                message(r, dy, zt).start()

        @pl.when(r == 0)
        def _():
            slab_piece((0, 1), quarter[0], 8, core, 0, x_left).wait_recv()
            slab_piece((1, 1), quarter[0], 8, core, 2, x_right).start()
            slab_piece((1, 1), quarter[0], 8, core, 3, x_left).start()
            slab_piece((1, 1), quarter[0], 8, core, 6, sibling).start()

        @pl.when(r == 3)
        def _():
            slab_piece((1, 1), quarter[3], 8, core, 2, x_right).wait_recv()
            slab_piece((1, 1), quarter[3], 4, core, 4, x_right).start()
            slab_piece((1, 1), quarter[1], 8, core, 3, x_left).wait_recv()
            slab_piece((1, 1), quarter[1] + 4, 4, core, 5, x_left).start()
            slab_piece((1, 1), quarter[3], 8, core, 7, sibling).start()
            slab_piece((1, 1), quarter[1], 8, core, 8, sibling).start()

        return carry

    lax.fori_loop(0, NR, dress, 0)
    sent.append(slab_piece((1, 1), quarter[0], 8, core, 2, x_right))
    sent.append(slab_piece((1, 1), quarter[0], 8, core, 3, x_left))
    sent.append(slab_piece((1, 1), quarter[0], 8, core, 6, sibling))
    sent.append(slab_piece((1, 1), quarter[3], 4, core, 4, x_right))
    sent.append(slab_piece((1, 1), quarter[1] + 4, 4, core, 5, x_left))
    sent.append(slab_piece((1, 1), quarter[3], 8, core, 7, sibling))
    sent.append(slab_piece((1, 1), quarter[1], 8, core, 8, sibling))

    slab_piece((0, 0), 0, 32, 1 - core, 1, sibling).wait_recv()
    total[...] = jnp.zeros_like(total)

    def ladder(r, half_of):
        for dy in range(4):
            if spots[dy][0] == half_of:
                for kind in kinds((dy,)):
                    message(r, *kind).wait_recv()
        cs = pl.ds(r * per, per)
        rows = jnp.concatenate(
            [recv[half_of, :, r * per + c].reshape(128, BLK) for c in range(per)], axis=1
        )
        weights = slab[half_of, cs].reshape(per * BLK, BLK)
        total[half_of] += jnp.dot(rows, weights, preferred_element_type=F32)

    def ladder_first(r, carry):
        ladder(r, 0)
        return carry

    def ladder_second(r, carry):
        ladder(r, 1)
        return carry

    lax.fori_loop(0, NR - 1, ladder_first, 0)
    slab_piece((1, 1), quarter[2], 4, core, 4, x_right).wait_recv()
    slab_piece((1, 1), quarter[2] + 4, 4, core, 5, x_left).wait_recv()
    go(slab_piece((1, 1), quarter[2], 8, core, 9, sibling))
    for slot, q in ((6, 0), (7, 3), (8, 1), (9, 2)):
        slab_piece((1, 1), quarter[q], 8, 1 - core, slot, sibling).wait_recv()
    lax.fori_loop(0, NR - 1, ladder_second, 0)
    def home(which, place, side):
        at = device(x, (y + which) % 4, (z + 2 * place) % 4, side)
        land = (near, beyond)[place].at[which, core]
        rows = (pl.ds(0, 48), pl.ds(48, 16))[place]
        return pltpu.make_async_remote_copy(
            src_ref=result.at[which, side, :, rows], dst_ref=land,
            send_sem=fin_send.at[which, place, side], recv_sem=fin_recv.at[which, place, core],
            device_id=at, device_id_type=MESH,
        )

    for which in (1, 0):
        ladder(NR - 1, which)
        h = zl * 4 + (y + which) % 4
        value = jnp.where(lane < counts[h], total[which], 0.0).astype(BF16).reshape(2, 64, BLK)
        for side in range(2):
            result[which, side] = value[:, :, side * 128 : (side + 1) * 128]
        for place in (1, 0):
            for side in range(2):
                if which == 0 and place == 0:
                    @pl.when(core != side)
                    def _():
                        home(0, 0, side).start()
                else:
                    home(which, place, side).start()
    near[0, core] = result[0, core, :, 0:48]

    for copy in sent:
        copy.wait_send()

    def drain(r, carry):
        for dy, zt in kinds(range(4)):
            message(r, dy, zt).wait_send()
        return carry

    lax.fori_loop(0, NR, drain, 0)

    def arrival(which, place, side):
        land = (near, beyond)[place].at[which, side]
        rows = (pl.ds(0, 48), pl.ds(48, 16))[place]
        return pltpu.make_async_remote_copy(
            src_ref=result.at[which, side, :, rows], dst_ref=land,
            send_sem=fin_send.at[which, place, side], recv_sem=fin_recv.at[which, place, side],
            device_id=sibling, device_id_type=MESH,
        )

    for which in range(2):
        for place in range(2):
            for side in range(2):
                if which == 0 and place == 0:
                    @pl.when(core != side)
                    def _():
                        arrival(0, 0, side).wait()
                else:
                    arrival(which, place, side).wait()
    for which in range(2):
        for other in range(2):
            source = (y + ((0, 1), (3, 2))[which][other]) % 4
            for side in range(2):
                out_ref[zl, source, side] = near[which, side, other, 0:32]
                out_ref[1 - zl, source, side, 0:16] = near[which, side, other, 32:48]
                out_ref[1 - zl, source, side, 16:32] = beyond[which, side, other]


def body(amplitudes, cycle_inter, ladder_slab, irrep_counts, slab_irrep):
    any_spec = pl.BlockSpec(memory_space=pl.ANY)
    smem = pl.BlockSpec(memory_space=pltpu.SMEM)
    dma = pltpu.SemaphoreType.DMA
    block = lax.broadcasted_iota(jnp.int32, (3, 8), 1) ^ slab_irrep[0]
    row = lax.broadcasted_iota(jnp.int32, (3, 8), 0)
    table = jnp.where(row == 0, block, jnp.where(row == 1, block >> 2, block & 3))
    out = pl.pallas_call(
        kernel,
        out_shape=jax.ShapeDtypeStruct((2, 4, 2, 32, 128), BF16),
        in_specs=[any_spec, any_spec, any_spec, smem, smem],
        out_specs=pl.BlockSpec(memory_space=pltpu.VMEM),
        scratch_shapes=[
            pltpu.VMEM((32, 32, 2048), BF16),
            pltpu.VMEM((2, 1024, 128), F32),
            pltpu.VMEM((8, 32, 32, BLK), BF16),
        ]
        + [pltpu.VMEM((2, 4, 2, 4, 2, 16, w), BF16) for w in WIDTHS]
        + [
            pltpu.VMEM((2, 4, 32, 32, BLK), BF16),
            pltpu.VMEM((2, 2, 32, 64, BLK), BF16),
            pltpu.VMEM((2, 32, BLK, BLK), BF16),
            pltpu.VMEM((2, 128, BLK), F32),
            pltpu.VMEM((2, 2, 2, 64, 128), BF16),
            pltpu.VMEM((2, 2, 2, 48, 128), BF16),
            pltpu.VMEM((2, 2, 2, 16, 128), BF16),
            dma((5,)),
            dma((3, 18)),
            dma((3, 18)),
            dma((3, 4)),
            dma((3, 4)),
            dma((NR, 4, 3)),
            dma((NR, 4, 3)),
            dma((10,)),
            dma((10,)),
            dma((2, 2, 2)),
            dma((2, 2, 2)),
        ],
        compiler_params=pltpu.CompilerParams(
            collective_id=0, has_side_effects=True, vmem_limit_bytes=56 * 1024 * 1024
        ),
        cost_estimate=pl.CostEstimate(
            flops=11 * 10**9, bytes_accessed=7 * 10**6, transcendentals=0
        ),
    )(amplitudes, cycle_inter.T, ladder_slab, irrep_counts, table)
    return out.reshape(512, 128)


def solution(mesh):
    placed = (
        P(("occ", "vir"), None, None),
        P(None, ("occ", "vir")),
        P(None, None, "vir"),
        P(),
        P(),
    )
    return jax.shard_map(
        body, mesh=mesh, in_specs=placed, out_specs=P("occ", "vir"), check_vma=False
    )
```

```python
import jax
import jax.numpy as jnp
from jax import lax
from jax.experimental import pallas as pl
from jax.experimental.pallas import tpu as pltpu
from jax.sharding import PartitionSpec as P

BLK = 256
WIDTHS = (768, 512, 768)
ORDERS = ("yzx", "zxy", "xyz")
NR = 4
MESH = pl.DeviceIdType.MESH
F32 = jnp.float32
BF16 = jnp.bfloat16
ALL = slice(None)


def device(x, y, z, core):
    return (z // 2 * 4 + x, z % 2 * 8 + y * 2 + core)


def kernel(
    amp_hbm, cyc_hbm, slab_hbm, counts, table, out_ref,
    raw, trans, amp, g0, g1, g2, dressed, recv, slab, total, result, near, beyond,
    local_sem, gather_send, gather_recv, sib_send, sib_recv, a2a_send, a2a_recv,
    slab_send, slab_recv, fin_send, fin_recv,
):
    occ, vir = lax.axis_index("occ"), lax.axis_index("vir")
    x, y, core = occ % 4, vir // 2 % 4, vir % 2
    zh, zl = occ // 4, vir // 8
    z = zh * 2 + zl
    gs = (g0, g1, g2)
    pos = {"x": x, "y": y, "z": z}
    sibling = device(x, y, z, 1 - core)
    z_inner = (z + 1 + 2 * zl) % 4
    z_outer = (z + 3 + 2 * zl) % 4
    z_of = (z, z_inner, z_outer)

    def neighbour(dim, step):
        at = dict(pos)
        at[dim] = (at[dim] + step) % 4
        return device(at["x"], at["y"], at["z"], core)

    load_amp = pltpu.make_async_copy(amp_hbm, raw, local_sem.at[0])
    load_amp.start()
    half = pl.ds(pl.multiple_of(core * 128, 128), 128)
    load_slab = pltpu.make_async_copy(slab_hbm, slab.at[0, :, :, half], local_sem.at[1])
    load_slab.start()
    offset = 0
    load_cyc = []
    for p in range(3):
        w = WIDTHS[p]
        load_cyc.append(
            pltpu.make_async_copy(
                cyc_hbm.at[:, pl.ds(offset, w)], gs[p].at[zh, x, zl, y, core], local_sem.at[2 + p]
            )
        )
        load_cyc[-1].start()
        offset += w

    barrier = pltpu.get_barrier_semaphore()
    greet = [sibling] + [neighbour(dim, step) for dim in "xyz" for step in (1, 3, 2)]
    for who in greet:
        pl.semaphore_signal(barrier, inc=1, device_id=who, device_id_type=MESH)
    pl.semaphore_wait(barrier, len(greet))

    def region(p, second, third, part, side):
        d1, d2, d3 = ORDERS[p]
        at = {d1: ALL if part is None else pl.ds(2 * part, 2), d2: second, d3: third}
        zhi, zlo = at["z"] // 2 if at["z"] is not ALL and d1 != "z" else ALL, ALL
        if d1 == "z":
            zhi = ALL if part is None else part
        elif at["z"] is not ALL:
            zlo = at["z"] % 2
        return gs[p].at[zhi, at["x"], zlo, at["y"], side]

    def pass_on(p, second, third, part, slot, who):
        ref = region(p, second, third, part, core)
        return pltpu.make_async_remote_copy(
            src_ref=ref, dst_ref=ref,
            send_sem=gather_send.at[p, slot], recv_sem=gather_recv.at[p, slot],
            device_id=who, device_id_type=MESH,
        )

    def to_sibling(p, second, third, slot, side):
        ref = region(p, second, third, None, side)
        return pltpu.make_async_remote_copy(
            src_ref=ref, dst_ref=ref,
            send_sem=sib_send.at[p, slot], recv_sem=sib_recv.at[p, slot],
            device_id=sibling, device_id_type=MESH,
        )

    sent = []

    def go(copy):
        copy.start()
        sent.append(copy)

    lane = lax.broadcasted_iota(jnp.int32, (1, BLK), 1)

    def transpose_block(k):
        cols = pl.ds(pl.multiple_of(k * BLK, BLK), BLK)
        block = raw[:, :, cols].astype(F32)
        block = jnp.where((lane < counts[k])[None], block, 0.0)
        block = block.reshape(1024, BLK)
        trans[0] = block[:, :128]
        trans[1] = block[:, 128:]

        def one(c, carry):
            rows = pl.ds(c, 32, stride=32)
            pair = [trans[0, rows, :], trans[1, rows, :]]
            amp[k, c] = jnp.concatenate(pair, axis=1).astype(BF16)
            return carry

        lax.fori_loop(0, 32, one, 0, unroll=4)

    def transpose_blocks(first, last):
        def one(k, carry):
            transpose_block(k)
            return carry

        lax.fori_loop(first, last, one, 0)

    def slab_piece(which, first, count, side, slot, who):
        lanes = pl.ds(pl.multiple_of(side * 128, 128), 128)
        src = slab.at[which[0], pl.ds(first, count), :, lanes]
        dst = slab.at[which[1], pl.ds(first, count), :, lanes]
        return pltpu.make_async_remote_copy(
            src_ref=src, dst_ref=dst, send_sem=slab_send.at[slot], recv_sem=slab_recv.at[slot],
            device_id=who, device_id_type=MESH,
        )

    quarter = [(x + i) % 4 * 8 for i in range(4)]
    x_right, x_left = neighbour("x", 1), neighbour("x", 3)

    def first(p, step, source):
        d1 = ORDERS[p][0]
        at = dict(pos)
        at[d1] = (at[d1] + source) % 4
        ref = gs[p].at[at["z"] // 2, at["x"], at["z"] % 2, at["y"], core]
        return pltpu.make_async_remote_copy(
            src_ref=ref, dst_ref=ref,
            send_sem=gather_send.at[p, step - 1], recv_sem=gather_recv.at[p, step - 1],
            device_id=neighbour(d1, step), device_id_type=MESH,
        )

    offsets = (0, 3, 1, 2)
    seconds = [[(pos[ORDERS[p][1]] + i) % 4 for i in offsets] for p in range(3)]
    thirds = [[(pos[ORDERS[p][2]] + i) % 4 for i in offsets] for p in range(3)]
    steps = (1, 3, 2)

    def along_second(p, i, slot):
        who = neighbour(ORDERS[p][1], steps[slot])
        return pass_on(p, seconds[p][i], thirds[p][0], None, 3 + slot, who)

    def along_third(p, sub, i, slot):
        who = neighbour(ORDERS[p][2], steps[slot])
        return pass_on(p, seconds[p][sub], thirds[p][i], None, 6 + 3 * sub + slot, who)

    def spread(p, sub):
        for slot in range(3):
            go(along_third(p, sub, 0, slot))

    def slab_fetch(first, slot):
        lanes = pl.ds(pl.multiple_of(core * 128, 128), 128)
        return pltpu.make_async_remote_copy(
            src_ref=slab_hbm.at[pl.ds(first, 8)], dst_ref=slab.at[1, pl.ds(first, 8), :, lanes],
            send_sem=slab_send.at[slot], recv_sem=slab_recv.at[slot],
            device_id=neighbour("y", 3), device_id_type=MESH,
        )

    for p in range(3):
        load_cyc[p].wait()
        for step in steps:
            go(first(p, step, 0))
    load_amp.wait()
    transpose_blocks(0, 1)
    for p in range(3):
        for step in steps:
            first(p, step, 4 - step).wait_recv()
        for slot in range(3):
            go(along_second(p, 0, slot))
        spread(p, 0)
    load_slab.wait()
    go(slab_piece((0, 0), 0, 32, core, 1, sibling))
    transpose_blocks(1, 3)
    for slot in range(3):
        for p in range(3):
            along_second(p, slot + 1, slot).wait_recv()
            spread(p, slot + 1)
    go(slab_fetch(quarter[0], 0))
    transpose_blocks(3, 8)
    for sub in range(4):
        for p in range(3):
            for slot in range(3):
                along_third(p, sub, slot + 1, slot).wait_recv()
            go(to_sibling(p, seconds[p][sub], ALL, sub, core))
    for p in range(3):
        for sub in range(4):
            to_sibling(p, seconds[p][sub], ALL, sub, 1 - core).wait_recv()
    per = 32 // NR
    spots = ((0, 0), (1, 0), (1, 1), (0, 1))
    y_of = (y, y, (y + 1) % 4, (y + 3) % 4)

    def message(r, dy, zt):
        cs = pl.ds(r * per, per)
        src = dressed.at[int(zt > 0), dy, cs]
        dst = recv.at[spots[dy][0], spots[dy][1], cs]
        if zt == 0:
            dst = recv.at[spots[dy][0], spots[dy][1], cs, pl.ds(0, 32)]
        else:
            src = dressed.at[1, dy, cs, pl.ds(16 * zt - 16, 16)]
            dst = recv.at[spots[dy][0], spots[dy][1], cs, pl.ds(16 + 16 * zt, 16)]
        return pltpu.make_async_remote_copy(
            src_ref=src, dst_ref=dst,
            send_sem=a2a_send.at[r, dy, zt], recv_sem=a2a_recv.at[r, dy, zt],
            device_id=device(x, y_of[dy], z_of[zt], core), device_id_type=MESH,
        )

    def kinds(dys):
        return [(dy, zt) for zt in (1, 2, 0) for dy in dys if dy > 1 or zt > 0]

    def dress(r, carry):
        cs = pl.ds(r * per, per)
        for dys in ((0, 2), (1, 3)):
            blocks = [(dz, dy) for dy in dys for dz in range(2)]
            tables = []
            for dz, dy in blocks:
                h = (zl + dz) % 2 * 4 + (y + dy) % 4
                tables.append([table[i, h] for i in range(3)])
            weights = jnp.concatenate(
                [
                    jnp.concatenate(
                        [g[t[1], t[2]].reshape(BLK, w) for g, w in zip(gs, WIDTHS)], axis=1
                    )
                    for t in tables
                ],
                axis=0,
            )
            rows = jnp.concatenate([amp[i, cs].reshape(per * 32, BLK) for i in range(8)], axis=1)
            values = lax.dot_general(
                rows, weights, (((1,), (1,)), ((), ())), preferred_element_type=F32
            )
            for i, (dz, dy) in enumerate(blocks):
                value = values[:, i * BLK : (i + 1) * BLK]
                value += amp[tables[i][0], cs].reshape(per * 32, BLK).astype(F32)
                value = jnp.where(lane < counts[tables[i][0]], value, 0.0).astype(BF16)
                value = value.reshape(per, 32, BLK)
                if dz == 0 and dy < 2:
                    recv[spots[dy][0], spots[dy][1], cs, 0:32] = value
                else:
                    dressed[dz, dy, cs] = value
            for dy, zt in kinds(dys):
                message(r, dy, zt).start()

        @pl.when(r == 0)
        def _():
            slab_piece((0, 1), quarter[0], 8, core, 0, x_left).wait_recv()
            slab_piece((1, 1), quarter[0], 8, core, 2, x_right).start()
            slab_piece((1, 1), quarter[0], 8, core, 3, x_left).start()
            slab_piece((1, 1), quarter[0], 8, core, 6, sibling).start()

        @pl.when(r == 3)
        def _():
            slab_piece((1, 1), quarter[3], 8, core, 2, x_right).wait_recv()
            slab_piece((1, 1), quarter[3], 4, core, 4, x_right).start()
            slab_piece((1, 1), quarter[1], 8, core, 3, x_left).wait_recv()
            slab_piece((1, 1), quarter[1] + 4, 4, core, 5, x_left).start()
            slab_piece((1, 1), quarter[3], 8, core, 7, sibling).start()
            slab_piece((1, 1), quarter[1], 8, core, 8, sibling).start()

        return carry

    lax.fori_loop(0, NR, dress, 0)
    sent.append(slab_piece((1, 1), quarter[0], 8, core, 2, x_right))
    sent.append(slab_piece((1, 1), quarter[0], 8, core, 3, x_left))
    sent.append(slab_piece((1, 1), quarter[0], 8, core, 6, sibling))
    sent.append(slab_piece((1, 1), quarter[3], 4, core, 4, x_right))
    sent.append(slab_piece((1, 1), quarter[1] + 4, 4, core, 5, x_left))
    sent.append(slab_piece((1, 1), quarter[3], 8, core, 7, sibling))
    sent.append(slab_piece((1, 1), quarter[1], 8, core, 8, sibling))

    slab_piece((0, 0), 0, 32, 1 - core, 1, sibling).wait_recv()
    total[...] = jnp.zeros_like(total)

    def ladder(r, half_of):
        for dy in range(4):
            if spots[dy][0] == half_of:
                for kind in kinds((dy,)):
                    message(r, *kind).wait_recv()
        cs = pl.ds(r * per, per)
        rows = jnp.concatenate(
            [recv[half_of, :, r * per + c].reshape(128, BLK) for c in range(per)], axis=1
        )
        weights = slab[half_of, cs].reshape(per * BLK, BLK)
        total[half_of] += jnp.dot(rows, weights, preferred_element_type=F32)

    def ladder_first(r, carry):
        ladder(r, 0)
        return carry

    def ladder_second(r, carry):
        ladder(r, 1)
        return carry

    lax.fori_loop(0, NR - 1, ladder_first, 0)
    slab_piece((1, 1), quarter[2], 4, core, 4, x_right).wait_recv()
    slab_piece((1, 1), quarter[2] + 4, 4, core, 5, x_left).wait_recv()
    go(slab_piece((1, 1), quarter[2], 8, core, 9, sibling))
    for slot, q in ((6, 0), (7, 3), (8, 1), (9, 2)):
        slab_piece((1, 1), quarter[q], 8, 1 - core, slot, sibling).wait_recv()
    lax.fori_loop(0, NR - 1, ladder_second, 0)
    def home(which, place, side):
        at = device(x, (y + which) % 4, (z + 2 * place) % 4, side)
        land = (near, beyond)[place].at[which, core]
        rows = (pl.ds(0, 48), pl.ds(48, 16))[place]
        return pltpu.make_async_remote_copy(
            src_ref=result.at[which, side, :, rows], dst_ref=land,
            send_sem=fin_send.at[which, place, side], recv_sem=fin_recv.at[which, place, core],
            device_id=at, device_id_type=MESH,
        )

    for which in (1, 0):
        ladder(NR - 1, which)
        h = zl * 4 + (y + which) % 4
        value = jnp.where(lane < counts[h], total[which], 0.0).astype(BF16).reshape(2, 64, BLK)
        for side in range(2):
            result[which, side] = value[:, :, side * 128 : (side + 1) * 128]
        for place in (1, 0):
            for side in range(2):
                if which == 0 and place == 0:
                    @pl.when(core != side)
                    def _():
                        home(0, 0, side).start()
                else:
                    home(which, place, side).start()
    near[0, core] = result[0, core, :, 0:48]

    for copy in sent:
        copy.wait_send()

    def drain(r, carry):
        for dy, zt in kinds(range(4)):
            message(r, dy, zt).wait_send()
        return carry

    lax.fori_loop(0, NR, drain, 0)

    def arrival(which, place, side):
        land = (near, beyond)[place].at[which, side]
        rows = (pl.ds(0, 48), pl.ds(48, 16))[place]
        return pltpu.make_async_remote_copy(
            src_ref=result.at[which, side, :, rows], dst_ref=land,
            send_sem=fin_send.at[which, place, side], recv_sem=fin_recv.at[which, place, side],
            device_id=sibling, device_id_type=MESH,
        )

    for which in range(2):
        for place in range(2):
            for side in range(2):
                if which == 0 and place == 0:
                    @pl.when(core != side)
                    def _():
                        arrival(0, 0, side).wait()
                else:
                    arrival(which, place, side).wait()
    for which in range(2):
        for other in range(2):
            source = (y + ((0, 1), (3, 2))[which][other]) % 4
            for side in range(2):
                out_ref[zl, source, side] = near[which, side, other, 0:32]
                out_ref[1 - zl, source, side, 0:16] = near[which, side, other, 32:48]
                out_ref[1 - zl, source, side, 16:32] = beyond[which, side, other]


def body(amplitudes, cycle_inter, ladder_slab, irrep_counts, slab_irrep):
    any_spec = pl.BlockSpec(memory_space=pl.ANY)
    smem = pl.BlockSpec(memory_space=pltpu.SMEM)
    dma = pltpu.SemaphoreType.DMA
    block = lax.broadcasted_iota(jnp.int32, (3, 8), 1) ^ slab_irrep[0]
    row = lax.broadcasted_iota(jnp.int32, (3, 8), 0)
    table = jnp.where(row == 0, block, jnp.where(row == 1, block >> 2, block & 3))
    out = pl.pallas_call(
        kernel,
        out_shape=jax.ShapeDtypeStruct((2, 4, 2, 32, 128), BF16),
        in_specs=[any_spec, any_spec, any_spec, smem, smem],
        out_specs=pl.BlockSpec(memory_space=pltpu.VMEM),
        scratch_shapes=[
            pltpu.VMEM((32, 32, 2048), BF16),
            pltpu.VMEM((2, 1024, 128), F32),
            pltpu.VMEM((8, 32, 32, BLK), BF16),
        ]
        + [pltpu.VMEM((2, 4, 2, 4, 2, 16, w), BF16) for w in WIDTHS]
        + [
            pltpu.VMEM((2, 4, 32, 32, BLK), BF16),
            pltpu.VMEM((2, 2, 32, 64, BLK), BF16),
            pltpu.VMEM((2, 32, BLK, BLK), BF16),
            pltpu.VMEM((2, 128, BLK), F32),
            pltpu.VMEM((2, 2, 2, 64, 128), BF16),
            pltpu.VMEM((2, 2, 2, 48, 128), BF16),
            pltpu.VMEM((2, 2, 2, 16, 128), BF16),
            dma((5,)),
            dma((3, 18)),
            dma((3, 18)),
            dma((3, 4)),
            dma((3, 4)),
            dma((NR, 4, 3)),
            dma((NR, 4, 3)),
            dma((10,)),
            dma((10,)),
            dma((2, 2, 2)),
            dma((2, 2, 2)),
        ],
        compiler_params=pltpu.CompilerParams(
            collective_id=0, has_side_effects=True, vmem_limit_bytes=56 * 1024 * 1024
        ),
        cost_estimate=pl.CostEstimate(
            flops=11 * 10**9, bytes_accessed=7 * 10**6, transcendentals=0
        ),
    )(amplitudes, cycle_inter.T, ladder_slab, irrep_counts, table)
    return out.reshape(512, 128)


def solution(mesh):
    placed = (
        P(("occ", "vir"), None, None),
        P(None, ("occ", "vir")),
        P(None, None, "vir"),
        P(),
        P(),
    )
    return jax.shard_map(
        body, mesh=mesh, in_specs=placed, out_specs=P("occ", "vir"), check_vma=False
    )
```

```python
import jax
import jax.numpy as jnp
from jax import lax
from jax.experimental import pallas as pl
from jax.experimental.pallas import tpu as pltpu
from jax.sharding import PartitionSpec as P

BLK = 256
WIDTHS = (768, 512, 768)
ORDERS = ("yzx", "zxy", "xyz")
NR = 4
MESH = pl.DeviceIdType.MESH
F32 = jnp.float32
BF16 = jnp.bfloat16
ALL = slice(None)


def device(x, y, z, core):
    return (z // 2 * 4 + x, z % 2 * 8 + y * 2 + core)


def kernel(
    amp_hbm, cyc_hbm, slab_hbm, counts, table, out_ref,
    raw, trans, amp, g0, g1, g2, dressed, recv, slab, total, result, near, beyond,
    local_sem, gather_send, gather_recv, sib_send, sib_recv, a2a_send, a2a_recv,
    slab_send, slab_recv, fin_send, fin_recv,
):
    occ, vir = lax.axis_index("occ"), lax.axis_index("vir")
    x, y, core = occ % 4, vir // 2 % 4, vir % 2
    zh, zl = occ // 4, vir // 8
    z = zh * 2 + zl
    gs = (g0, g1, g2)
    pos = {"x": x, "y": y, "z": z}
    sibling = device(x, y, z, 1 - core)
    z_inner = (z + 1 + 2 * zl) % 4
    z_outer = (z + 3 + 2 * zl) % 4
    z_of = (z, z_inner, z_outer)

    def neighbour(dim, step):
        at = dict(pos)
        at[dim] = (at[dim] + step) % 4
        return device(at["x"], at["y"], at["z"], core)

    load_amp = pltpu.make_async_copy(amp_hbm, raw, local_sem.at[0])
    load_amp.start()
    half = pl.ds(pl.multiple_of(core * 128, 128), 128)
    load_slab = pltpu.make_async_copy(slab_hbm, slab.at[0, :, :, half], local_sem.at[1])
    load_slab.start()
    offset = 0
    load_cyc = []
    for p in range(3):
        w = WIDTHS[p]
        load_cyc.append(
            pltpu.make_async_copy(
                cyc_hbm.at[:, pl.ds(offset, w)], gs[p].at[zh, x, zl, y, core], local_sem.at[2 + p]
            )
        )
        load_cyc[-1].start()
        offset += w

    barrier = pltpu.get_barrier_semaphore()
    greet = [sibling] + [neighbour(dim, step) for dim in "xyz" for step in (1, 3, 2)]
    for who in greet:
        pl.semaphore_signal(barrier, inc=1, device_id=who, device_id_type=MESH)
    pl.semaphore_wait(barrier, len(greet))

    def region(p, second, third, part, side):
        d1, d2, d3 = ORDERS[p]
        at = {d1: ALL if part is None else pl.ds(2 * part, 2), d2: second, d3: third}
        zhi, zlo = at["z"] // 2 if at["z"] is not ALL and d1 != "z" else ALL, ALL
        if d1 == "z":
            zhi = ALL if part is None else part
        elif at["z"] is not ALL:
            zlo = at["z"] % 2
        return gs[p].at[zhi, at["x"], zlo, at["y"], side]

    def pass_on(p, second, third, part, slot, who):
        ref = region(p, second, third, part, core)
        return pltpu.make_async_remote_copy(
            src_ref=ref, dst_ref=ref,
            send_sem=gather_send.at[p, slot], recv_sem=gather_recv.at[p, slot],
            device_id=who, device_id_type=MESH,
        )

    def to_sibling(p, second, third, slot, side):
        ref = region(p, second, third, None, side)
        return pltpu.make_async_remote_copy(
            src_ref=ref, dst_ref=ref,
            send_sem=sib_send.at[p, slot], recv_sem=sib_recv.at[p, slot],
            device_id=sibling, device_id_type=MESH,
        )

    sent = []

    def go(copy):
        copy.start()
        sent.append(copy)

    lane = lax.broadcasted_iota(jnp.int32, (1, BLK), 1)

    def transpose_block(k):
        cols = pl.ds(pl.multiple_of(k * BLK, BLK), BLK)
        block = raw[:, :, cols].astype(F32)
        block = jnp.where((lane < counts[k])[None], block, 0.0)
        block = block.reshape(1024, BLK)
        trans[0] = block[:, :128]
        trans[1] = block[:, 128:]

        def one(c, carry):
            rows = pl.ds(c, 32, stride=32)
            pair = [trans[0, rows, :], trans[1, rows, :]]
            amp[k, c] = jnp.concatenate(pair, axis=1).astype(BF16)
            return carry

        lax.fori_loop(0, 32, one, 0, unroll=4)

    def transpose_blocks(first, last):
        def one(k, carry):
            transpose_block(k)
            return carry

        lax.fori_loop(first, last, one, 0)

    def slab_piece(which, first, count, side, slot, who):
        lanes = pl.ds(pl.multiple_of(side * 128, 128), 128)
        src = slab.at[which[0], pl.ds(first, count), :, lanes]
        dst = slab.at[which[1], pl.ds(first, count), :, lanes]
        return pltpu.make_async_remote_copy(
            src_ref=src, dst_ref=dst, send_sem=slab_send.at[slot], recv_sem=slab_recv.at[slot],
            device_id=who, device_id_type=MESH,
        )

    quarter = [(x + i) % 4 * 8 for i in range(4)]
    x_right, x_left = neighbour("x", 1), neighbour("x", 3)

    def first(p, step, source):
        d1 = ORDERS[p][0]
        at = dict(pos)
        at[d1] = (at[d1] + source) % 4
        ref = gs[p].at[at["z"] // 2, at["x"], at["z"] % 2, at["y"], core]
        return pltpu.make_async_remote_copy(
            src_ref=cyc_hbm.at[:, pl.ds(sum(WIDTHS[:p]), WIDTHS[p])], dst_ref=ref,
            send_sem=gather_send.at[p, step - 1], recv_sem=gather_recv.at[p, step - 1],
            device_id=neighbour(d1, step), device_id_type=MESH,
        )

    offsets = (0, 3, 1, 2)
    seconds = [[(pos[ORDERS[p][1]] + i) % 4 for i in offsets] for p in range(3)]
    thirds = [[(pos[ORDERS[p][2]] + i) % 4 for i in offsets] for p in range(3)]
    steps = (1, 3, 2)

    def along_second(p, i, slot):
        who = neighbour(ORDERS[p][1], steps[slot])
        return pass_on(p, seconds[p][i], thirds[p][0], None, 3 + slot, who)

    def along_third(p, sub, i, slot):
        who = neighbour(ORDERS[p][2], steps[slot])
        return pass_on(p, seconds[p][sub], thirds[p][i], None, 6 + 3 * sub + slot, who)

    def spread(p, sub):
        for slot in range(3):
            go(along_third(p, sub, 0, slot))

    def slab_fetch(first, slot):
        lanes = pl.ds(pl.multiple_of(core * 128, 128), 128)
        return pltpu.make_async_remote_copy(
            src_ref=slab_hbm.at[pl.ds(first, 8)], dst_ref=slab.at[1, pl.ds(first, 8), :, lanes],
            send_sem=slab_send.at[slot], recv_sem=slab_recv.at[slot],
            device_id=neighbour("y", 3), device_id_type=MESH,
        )

    for p in range(3):
        for step in steps:
            go(first(p, step, 0))
    for copy in load_cyc:
        copy.wait()
    load_amp.wait()
    transpose_blocks(0, 1)
    for p in range(3):
        for step in steps:
            first(p, step, 4 - step).wait_recv()
        for slot in range(3):
            go(along_second(p, 0, slot))
        spread(p, 0)
    load_slab.wait()
    go(slab_piece((0, 0), 0, 32, core, 1, sibling))
    transpose_blocks(1, 3)
    for slot in range(3):
        for p in range(3):
            along_second(p, slot + 1, slot).wait_recv()
            spread(p, slot + 1)
    go(slab_fetch(quarter[0], 0))
    transpose_blocks(3, 8)
    for sub in range(3):
        for p in range(3):
            for slot in range(3):
                along_third(p, sub, slot + 1, slot).wait_recv()
            go(to_sibling(p, seconds[p][sub], ALL, sub, core))
            if sub == 0:
                go(to_sibling(p, seconds[p][3], thirds[p][0], 3, core))
    for slot in range(3):
        for p in range(3):
            along_third(p, 3, slot + 1, slot).wait_recv()
            go(to_sibling(p, seconds[p][3], thirds[p][slot + 1], 4 + slot, core))
    for p in range(3):
        for sub in range(3):
            to_sibling(p, seconds[p][sub], ALL, sub, 1 - core).wait_recv()
        for i in range(4):
            to_sibling(p, seconds[p][3], thirds[p][i], 3 + i, 1 - core).wait_recv()

    per = 32 // NR
    spots = ((0, 0), (1, 0), (1, 1), (0, 1))
    y_of = (y, y, (y + 1) % 4, (y + 3) % 4)

    def message(r, dy, zt):
        cs = pl.ds(r * per, per)
        src = dressed.at[int(zt > 0), dy, cs]
        dst = recv.at[spots[dy][0], spots[dy][1], cs]
        if zt == 0:
            dst = recv.at[spots[dy][0], spots[dy][1], cs, pl.ds(0, 32)]
        else:
            src = dressed.at[1, dy, cs, pl.ds(16 * zt - 16, 16)]
            dst = recv.at[spots[dy][0], spots[dy][1], cs, pl.ds(16 + 16 * zt, 16)]
        return pltpu.make_async_remote_copy(
            src_ref=src, dst_ref=dst,
            send_sem=a2a_send.at[r, dy, zt], recv_sem=a2a_recv.at[r, dy, zt],
            device_id=device(x, y_of[dy], z_of[zt], core), device_id_type=MESH,
        )

    def kinds(dys):
        return [(dy, zt) for zt in (1, 2, 0) for dy in dys if dy > 1 or zt > 0]

    def dress(r, carry):
        cs = pl.ds(r * per, per)
        for dys in ((0, 2), (1, 3)):
            blocks = [(dz, dy) for dy in dys for dz in range(2)]
            tables = []
            for dz, dy in blocks:
                h = (zl + dz) % 2 * 4 + (y + dy) % 4
                tables.append([table[i, h] for i in range(3)])
            weights = jnp.concatenate(
                [
                    jnp.concatenate(
                        [g[t[1], t[2]].reshape(BLK, w) for g, w in zip(gs, WIDTHS)], axis=1
                    )
                    for t in tables
                ],
                axis=0,
            )
            rows = jnp.concatenate([amp[i, cs].reshape(per * 32, BLK) for i in range(8)], axis=1)
            values = lax.dot_general(
                rows, weights, (((1,), (1,)), ((), ())), preferred_element_type=F32
            )
            for i, (dz, dy) in enumerate(blocks):
                value = values[:, i * BLK : (i + 1) * BLK]
                value += amp[tables[i][0], cs].reshape(per * 32, BLK).astype(F32)
                value = jnp.where(lane < counts[tables[i][0]], value, 0.0).astype(BF16)
                value = value.reshape(per, 32, BLK)
                if dz == 0 and dy < 2:
                    recv[spots[dy][0], spots[dy][1], cs, 0:32] = value
                else:
                    dressed[dz, dy, cs] = value
            for dy, zt in kinds(dys):
                message(r, dy, zt).start()

        @pl.when(r == 0)
        def _():
            slab_piece((0, 1), quarter[0], 8, core, 0, x_left).wait_recv()
            slab_piece((1, 1), quarter[0], 8, core, 2, x_right).start()
            slab_piece((1, 1), quarter[0], 8, core, 3, x_left).start()
            slab_piece((1, 1), quarter[0], 8, core, 6, sibling).start()

        @pl.when(r == 3)
        def _():
            slab_piece((1, 1), quarter[3], 8, core, 2, x_right).wait_recv()
            slab_piece((1, 1), quarter[3], 4, core, 4, x_right).start()
            slab_piece((1, 1), quarter[1], 8, core, 3, x_left).wait_recv()
            slab_piece((1, 1), quarter[1] + 4, 4, core, 5, x_left).start()
            slab_piece((1, 1), quarter[3], 8, core, 7, sibling).start()
            slab_piece((1, 1), quarter[1], 8, core, 8, sibling).start()

        return carry

    lax.fori_loop(0, NR, dress, 0)
    sent.append(slab_piece((1, 1), quarter[0], 8, core, 2, x_right))
    sent.append(slab_piece((1, 1), quarter[0], 8, core, 3, x_left))
    sent.append(slab_piece((1, 1), quarter[0], 8, core, 6, sibling))
    sent.append(slab_piece((1, 1), quarter[3], 4, core, 4, x_right))
    sent.append(slab_piece((1, 1), quarter[1] + 4, 4, core, 5, x_left))
    sent.append(slab_piece((1, 1), quarter[3], 8, core, 7, sibling))
    sent.append(slab_piece((1, 1), quarter[1], 8, core, 8, sibling))

    slab_piece((0, 0), 0, 32, 1 - core, 1, sibling).wait_recv()
    total[...] = jnp.zeros_like(total)

    def ladder(r, half_of):
        for dy in range(4):
            if spots[dy][0] == half_of:
                for kind in kinds((dy,)):
                    message(r, *kind).wait_recv()
        cs = pl.ds(r * per, per)
        rows = jnp.concatenate(
            [recv[half_of, :, r * per + c].reshape(128, BLK) for c in range(per)], axis=1
        )
        weights = slab[half_of, cs].reshape(per * BLK, BLK)
        total[half_of] += jnp.dot(rows, weights, preferred_element_type=F32)

    def ladder_first(r, carry):
        ladder(r, 0)
        return carry

    def ladder_second(r, carry):
        ladder(r, 1)
        return carry

    lax.fori_loop(0, NR - 1, ladder_first, 0)
    slab_piece((1, 1), quarter[2], 4, core, 4, x_right).wait_recv()
    slab_piece((1, 1), quarter[2] + 4, 4, core, 5, x_left).wait_recv()
    go(slab_piece((1, 1), quarter[2], 8, core, 9, sibling))
    for slot, q in ((6, 0), (7, 3), (8, 1), (9, 2)):
        slab_piece((1, 1), quarter[q], 8, 1 - core, slot, sibling).wait_recv()
    lax.fori_loop(0, NR - 1, ladder_second, 0)

    def drain(r, carry):
        for dy, zt in kinds(range(4)):
            message(r, dy, zt).wait_send()
        return carry

    for copy in sent:
        copy.wait_send()
    lax.fori_loop(0, NR - 1, drain, 0)

    def home(which, place, side):
        at = device(x, (y + which) % 4, (z + 2 * place) % 4, side)
        land = (near, beyond)[place].at[which, core]
        rows = (pl.ds(0, 48), pl.ds(48, 16))[place]
        return pltpu.make_async_remote_copy(
            src_ref=result.at[which, side, :, rows], dst_ref=land,
            send_sem=fin_send.at[which, place, side], recv_sem=fin_recv.at[which, place, core],
            device_id=at, device_id_type=MESH,
        )

    for which in (1, 0):
        ladder(NR - 1, which)
        h = zl * 4 + (y + which) % 4
        value = jnp.where(lane < counts[h], total[which], 0.0).astype(BF16).reshape(2, 64, BLK)
        for side in range(2):
            result[which, side] = value[:, :, side * 128 : (side + 1) * 128]
        for place in (1, 0):
            for side in range(2):
                if which == 0 and place == 0:
                    @pl.when(core != side)
                    def _():
                        home(0, 0, side).start()
                else:
                    home(which, place, side).start()
    near[0, core] = result[0, core, :, 0:48]

    drain(NR - 1, 0)

    def arrival(which, place, side):
        land = (near, beyond)[place].at[which, side]
        rows = (pl.ds(0, 48), pl.ds(48, 16))[place]
        return pltpu.make_async_remote_copy(
            src_ref=result.at[which, side, :, rows], dst_ref=land,
            send_sem=fin_send.at[which, place, side], recv_sem=fin_recv.at[which, place, side],
            device_id=sibling, device_id_type=MESH,
        )

    for which in range(2):
        for place in range(2):
            for side in range(2):
                if which == 0 and place == 0:
                    @pl.when(core != side)
                    def _():
                        arrival(0, 0, side).wait()
                else:
                    arrival(which, place, side).wait()
    for which in range(2):
        for other in range(2):
            source = (y + ((0, 1), (3, 2))[which][other]) % 4
            for side in range(2):
                out_ref[zl, source, side] = near[which, side, other, 0:32]
                out_ref[1 - zl, source, side, 0:16] = near[which, side, other, 32:48]
                out_ref[1 - zl, source, side, 16:32] = beyond[which, side, other]


def body(amplitudes, cycle_inter, ladder_slab, irrep_counts, slab_irrep):
    any_spec = pl.BlockSpec(memory_space=pl.ANY)
    smem = pl.BlockSpec(memory_space=pltpu.SMEM)
    dma = pltpu.SemaphoreType.DMA
    block = lax.broadcasted_iota(jnp.int32, (3, 8), 1) ^ slab_irrep[0]
    row = lax.broadcasted_iota(jnp.int32, (3, 8), 0)
    table = jnp.where(row == 0, block, jnp.where(row == 1, block >> 2, block & 3))
    out = pl.pallas_call(
        kernel,
        out_shape=jax.ShapeDtypeStruct((2, 4, 2, 32, 128), BF16),
        in_specs=[any_spec, any_spec, any_spec, smem, smem],
        out_specs=pl.BlockSpec(memory_space=pltpu.VMEM),
        scratch_shapes=[
            pltpu.VMEM((32, 32, 2048), BF16),
            pltpu.VMEM((2, 1024, 128), F32),
            pltpu.VMEM((8, 32, 32, BLK), BF16),
        ]
        + [pltpu.VMEM((2, 4, 2, 4, 2, 16, w), BF16) for w in WIDTHS]
        + [
            pltpu.VMEM((2, 4, 32, 32, BLK), BF16),
            pltpu.VMEM((2, 2, 32, 64, BLK), BF16),
            pltpu.VMEM((2, 32, BLK, BLK), BF16),
            pltpu.VMEM((2, 128, BLK), F32),
            pltpu.VMEM((2, 2, 2, 64, 128), BF16),
            pltpu.VMEM((2, 2, 2, 48, 128), BF16),
            pltpu.VMEM((2, 2, 2, 16, 128), BF16),
            dma((5,)),
            dma((3, 18)),
            dma((3, 18)),
            dma((3, 7)),
            dma((3, 7)),
            dma((NR, 4, 3)),
            dma((NR, 4, 3)),
            dma((10,)),
            dma((10,)),
            dma((2, 2, 2)),
            dma((2, 2, 2)),
        ],
        compiler_params=pltpu.CompilerParams(
            collective_id=0, has_side_effects=True, vmem_limit_bytes=56 * 1024 * 1024
        ),
        cost_estimate=pl.CostEstimate(
            flops=11 * 10**9, bytes_accessed=7 * 10**6, transcendentals=0
        ),
    )(amplitudes, cycle_inter.T, ladder_slab, irrep_counts, table)
    return out.reshape(512, 128)


def solution(mesh):
    placed = (
        P(("occ", "vir"), None, None),
        P(None, ("occ", "vir")),
        P(None, None, "vir"),
        P(),
        P(),
    )
    return jax.shard_map(
        body, mesh=mesh, in_specs=placed, out_specs=P("occ", "vir"), check_vma=False
    )
```

```python
import jax
import jax.numpy as jnp
from jax import lax
from jax.experimental import pallas as pl
from jax.experimental.pallas import tpu as pltpu
from jax.sharding import PartitionSpec as P

BLK = 256
WIDTHS = (768, 512, 768)
ORDERS = ("yzx", "zxy", "xyz")
NR = 4
MESH = pl.DeviceIdType.MESH
F32 = jnp.float32
BF16 = jnp.bfloat16
ALL = slice(None)


def device(x, y, z, core):
    return (z // 2 * 4 + x, z % 2 * 8 + y * 2 + core)


def kernel(
    amp_hbm, cyc_hbm, slab_hbm, counts, table, out_ref,
    raw, trans, amp, g0, g1, g2, dressed, recv, slab, total, result, near, beyond,
    local_sem, gather_send, gather_recv, sib_send, sib_recv, a2a_send, a2a_recv,
    slab_send, slab_recv, fin_send, fin_recv,
):
    occ, vir = lax.axis_index("occ"), lax.axis_index("vir")
    x, y, core = occ % 4, vir // 2 % 4, vir % 2
    zh, zl = occ // 4, vir // 8
    z = zh * 2 + zl
    gs = (g0, g1, g2)
    pos = {"x": x, "y": y, "z": z}
    sibling = device(x, y, z, 1 - core)
    z_inner = (z + 1 + 2 * zl) % 4
    z_outer = (z + 3 + 2 * zl) % 4
    z_of = (z, z_inner, z_outer)

    def neighbour(dim, step):
        at = dict(pos)
        at[dim] = (at[dim] + step) % 4
        return device(at["x"], at["y"], at["z"], core)

    load_amp = pltpu.make_async_copy(amp_hbm, raw, local_sem.at[0])
    load_amp.start()
    half = pl.ds(pl.multiple_of(core * 128, 128), 128)
    load_slab = pltpu.make_async_copy(slab_hbm, slab.at[0, :, :, half], local_sem.at[1])
    load_slab.start()
    offset = 0
    load_cyc = []
    for p in range(3):
        w = WIDTHS[p]
        load_cyc.append(
            pltpu.make_async_copy(
                cyc_hbm.at[:, pl.ds(offset, w)], gs[p].at[zh, x, zl, y, core], local_sem.at[2 + p]
            )
        )
        load_cyc[-1].start()
        offset += w

    barrier = pltpu.get_barrier_semaphore()
    greet = [sibling] + [neighbour(dim, step) for dim in "xyz" for step in (1, 3, 2)]
    for who in greet:
        pl.semaphore_signal(barrier, inc=1, device_id=who, device_id_type=MESH)
    pl.semaphore_wait(barrier, len(greet))

    def region(p, second, third, part, side):
        d1, d2, d3 = ORDERS[p]
        at = {d1: ALL if part is None else pl.ds(2 * part, 2), d2: second, d3: third}
        zhi, zlo = at["z"] // 2 if at["z"] is not ALL and d1 != "z" else ALL, ALL
        if d1 == "z":
            zhi = ALL if part is None else part
        elif at["z"] is not ALL:
            zlo = at["z"] % 2
        return gs[p].at[zhi, at["x"], zlo, at["y"], side]

    def pass_on(p, second, third, part, slot, who):
        ref = region(p, second, third, part, core)
        return pltpu.make_async_remote_copy(
            src_ref=ref, dst_ref=ref,
            send_sem=gather_send.at[p, slot], recv_sem=gather_recv.at[p, slot],
            device_id=who, device_id_type=MESH,
        )

    def to_sibling(p, second, third, slot, side):
        ref = region(p, second, third, None, side)
        return pltpu.make_async_remote_copy(
            src_ref=ref, dst_ref=ref,
            send_sem=sib_send.at[p, slot], recv_sem=sib_recv.at[p, slot],
            device_id=sibling, device_id_type=MESH,
        )

    sent = []

    def go(copy):
        copy.start()
        sent.append(copy)

    lane = lax.broadcasted_iota(jnp.int32, (1, BLK), 1)

    def transpose_block(k):
        cols = pl.ds(pl.multiple_of(k * BLK, BLK), BLK)
        block = raw[:, :, cols].astype(F32)
        block = jnp.where((lane < counts[k])[None], block, 0.0)
        block = block.reshape(1024, BLK)
        trans[0] = block[:, :128]
        trans[1] = block[:, 128:]

        def one(c, carry):
            rows = pl.ds(c, 32, stride=32)
            pair = [trans[0, rows, :], trans[1, rows, :]]
            amp[k, c] = jnp.concatenate(pair, axis=1).astype(BF16)
            return carry

        lax.fori_loop(0, 32, one, 0, unroll=4)

    def transpose_blocks(first, last):
        def one(k, carry):
            transpose_block(k)
            return carry

        lax.fori_loop(first, last, one, 0)

    def slab_piece(which, first, count, side, slot, who):
        lanes = pl.ds(pl.multiple_of(side * 128, 128), 128)
        src = slab.at[which[0], pl.ds(first, count), :, lanes]
        dst = slab.at[which[1], pl.ds(first, count), :, lanes]
        return pltpu.make_async_remote_copy(
            src_ref=src, dst_ref=dst, send_sem=slab_send.at[slot], recv_sem=slab_recv.at[slot],
            device_id=who, device_id_type=MESH,
        )

    quarter = [(x + i) % 4 * 8 for i in range(4)]
    x_right, x_left = neighbour("x", 1), neighbour("x", 3)

    def first(p, step, source):
        d1 = ORDERS[p][0]
        at = dict(pos)
        at[d1] = (at[d1] + source) % 4
        ref = gs[p].at[at["z"] // 2, at["x"], at["z"] % 2, at["y"], core]
        return pltpu.make_async_remote_copy(
            src_ref=cyc_hbm.at[:, pl.ds(sum(WIDTHS[:p]), WIDTHS[p])], dst_ref=ref,
            send_sem=gather_send.at[p, step - 1], recv_sem=gather_recv.at[p, step - 1],
            device_id=neighbour(d1, step), device_id_type=MESH,
        )

    offsets = (0, 3, 1, 2)
    seconds = [[(pos[ORDERS[p][1]] + i) % 4 for i in offsets] for p in range(3)]
    thirds = [[(pos[ORDERS[p][2]] + i) % 4 for i in offsets] for p in range(3)]
    steps = (1, 3, 2)

    def along_second(p, i, slot):
        who = neighbour(ORDERS[p][1], steps[slot])
        return pass_on(p, seconds[p][i], thirds[p][0], None, 3 + slot, who)

    def along_third(p, sub, i, slot):
        who = neighbour(ORDERS[p][2], steps[slot])
        return pass_on(p, seconds[p][sub], thirds[p][i], None, 6 + 3 * sub + slot, who)

    def spread(p, sub):
        for slot in range(3):
            go(along_third(p, sub, 0, slot))

    def slab_fetch(first, slot):
        lanes = pl.ds(pl.multiple_of(core * 128, 128), 128)
        return pltpu.make_async_remote_copy(
            src_ref=slab_hbm.at[pl.ds(first, 8)], dst_ref=slab.at[1, pl.ds(first, 8), :, lanes],
            send_sem=slab_send.at[slot], recv_sem=slab_recv.at[slot],
            device_id=neighbour("y", 3), device_id_type=MESH,
        )

    for p in range(3):
        for step in steps:
            go(first(p, step, 0))
    for copy in load_cyc:
        copy.wait()
    for p in range(3):
        for step in steps:
            first(p, step, 4 - step).wait_recv()
        for slot in range(3):
            go(along_second(p, 0, slot))
        spread(p, 0)
    load_slab.wait()
    go(slab_piece((0, 0), 0, 32, core, 1, sibling))
    load_amp.wait()
    transpose_blocks(0, 3)
    for slot in range(3):
        for p in range(3):
            along_second(p, slot + 1, slot).wait_recv()
            spread(p, slot + 1)
    go(slab_fetch(quarter[0], 0))
    transpose_blocks(3, 8)
    for sub in range(3):
        for p in range(3):
            for slot in range(3):
                along_third(p, sub, slot + 1, slot).wait_recv()
            go(to_sibling(p, seconds[p][sub], ALL, sub, core))
            if sub == 0:
                go(to_sibling(p, seconds[p][3], thirds[p][0], 3, core))
    for slot in range(3):
        for p in range(3):
            along_third(p, 3, slot + 1, slot).wait_recv()
            go(to_sibling(p, seconds[p][3], thirds[p][slot + 1], 4 + slot, core))
    for p in range(3):
        for sub in range(3):
            to_sibling(p, seconds[p][sub], ALL, sub, 1 - core).wait_recv()
        for i in range(4):
            to_sibling(p, seconds[p][3], thirds[p][i], 3 + i, 1 - core).wait_recv()

    per = 32 // NR
    spots = ((0, 0), (1, 0), (1, 1), (0, 1))
    y_of = (y, y, (y + 1) % 4, (y + 3) % 4)

    def message(r, dy, zt):
        cs = pl.ds(r * per, per)
        src = dressed.at[int(zt > 0), dy, cs]
        dst = recv.at[spots[dy][0], spots[dy][1], cs]
        if zt == 0:
            dst = recv.at[spots[dy][0], spots[dy][1], cs, pl.ds(0, 32)]
        else:
            src = dressed.at[1, dy, cs, pl.ds(16 * zt - 16, 16)]
            dst = recv.at[spots[dy][0], spots[dy][1], cs, pl.ds(16 + 16 * zt, 16)]
        return pltpu.make_async_remote_copy(
            src_ref=src, dst_ref=dst,
            send_sem=a2a_send.at[r, dy, zt], recv_sem=a2a_recv.at[r, dy, zt],
            device_id=device(x, y_of[dy], z_of[zt], core), device_id_type=MESH,
        )

    def kinds(dys):
        return [(dy, zt) for zt in (1, 2, 0) for dy in dys if dy > 1 or zt > 0]

    def dress(r, carry):
        cs = pl.ds(r * per, per)
        for dys in ((0, 2), (1, 3)):
            blocks = [(dz, dy) for dy in dys for dz in range(2)]
            tables = []
            for dz, dy in blocks:
                h = (zl + dz) % 2 * 4 + (y + dy) % 4
                tables.append([table[i, h] for i in range(3)])
            weights = jnp.concatenate(
                [
                    jnp.concatenate(
                        [g[t[1], t[2]].reshape(BLK, w) for g, w in zip(gs, WIDTHS)], axis=1
                    )
                    for t in tables
                ],
                axis=0,
            )
            rows = jnp.concatenate([amp[i, cs].reshape(per * 32, BLK) for i in range(8)], axis=1)
            values = lax.dot_general(
                rows, weights, (((1,), (1,)), ((), ())), preferred_element_type=F32
            )
            for i, (dz, dy) in enumerate(blocks):
                value = values[:, i * BLK : (i + 1) * BLK]
                value += amp[tables[i][0], cs].reshape(per * 32, BLK).astype(F32)
                value = jnp.where(lane < counts[tables[i][0]], value, 0.0).astype(BF16)
                value = value.reshape(per, 32, BLK)
                if dz == 0 and dy < 2:
                    recv[spots[dy][0], spots[dy][1], cs, 0:32] = value
                else:
                    dressed[dz, dy, cs] = value
            for dy, zt in kinds(dys):
                message(r, dy, zt).start()

        @pl.when(r == 0)
        def _():
            slab_piece((0, 1), quarter[0], 8, core, 0, x_left).wait_recv()
            slab_piece((1, 1), quarter[0], 8, core, 2, x_right).start()
            slab_piece((1, 1), quarter[0], 8, core, 3, x_left).start()
            slab_piece((1, 1), quarter[0], 8, core, 6, sibling).start()

        @pl.when(r == 3)
        def _():
            slab_piece((1, 1), quarter[3], 8, core, 2, x_right).wait_recv()
            slab_piece((1, 1), quarter[3], 4, core, 4, x_right).start()
            slab_piece((1, 1), quarter[1], 8, core, 3, x_left).wait_recv()
            slab_piece((1, 1), quarter[1] + 4, 4, core, 5, x_left).start()
            slab_piece((1, 1), quarter[3], 8, core, 7, sibling).start()
            slab_piece((1, 1), quarter[1], 8, core, 8, sibling).start()

        return carry

    lax.fori_loop(0, NR, dress, 0)
    sent.append(slab_piece((1, 1), quarter[0], 8, core, 2, x_right))
    sent.append(slab_piece((1, 1), quarter[0], 8, core, 3, x_left))
    sent.append(slab_piece((1, 1), quarter[0], 8, core, 6, sibling))
    sent.append(slab_piece((1, 1), quarter[3], 4, core, 4, x_right))
    sent.append(slab_piece((1, 1), quarter[1] + 4, 4, core, 5, x_left))
    sent.append(slab_piece((1, 1), quarter[3], 8, core, 7, sibling))
    sent.append(slab_piece((1, 1), quarter[1], 8, core, 8, sibling))

    slab_piece((0, 0), 0, 32, 1 - core, 1, sibling).wait_recv()
    total[...] = jnp.zeros_like(total)

    def ladder(r, half_of):
        for dy in range(4):
            if spots[dy][0] == half_of:
                for kind in kinds((dy,)):
                    message(r, *kind).wait_recv()
        cs = pl.ds(r * per, per)
        rows = jnp.concatenate(
            [recv[half_of, :, r * per + c].reshape(128, BLK) for c in range(per)], axis=1
        )
        weights = slab[half_of, cs].reshape(per * BLK, BLK)
        total[half_of] += jnp.dot(rows, weights, preferred_element_type=F32)

    def ladder_first(r, carry):
        ladder(r, 0)
        return carry

    def ladder_second(r, carry):
        ladder(r, 1)
        return carry

    lax.fori_loop(0, NR - 1, ladder_first, 0)
    slab_piece((1, 1), quarter[2], 4, core, 4, x_right).wait_recv()
    slab_piece((1, 1), quarter[2] + 4, 4, core, 5, x_left).wait_recv()
    go(slab_piece((1, 1), quarter[2], 8, core, 9, sibling))
    for slot, q in ((6, 0), (7, 3), (8, 1), (9, 2)):
        slab_piece((1, 1), quarter[q], 8, 1 - core, slot, sibling).wait_recv()
    lax.fori_loop(0, NR - 1, ladder_second, 0)

    def drain(r, carry):
        for dy, zt in kinds(range(4)):
            message(r, dy, zt).wait_send()
        return carry

    for copy in sent:
        copy.wait_send()
    lax.fori_loop(0, NR - 1, drain, 0)

    def home(which, place, side):
        at = device(x, (y + which) % 4, (z + 2 * place) % 4, side)
        land = (near, beyond)[place].at[which, core]
        rows = (pl.ds(0, 48), pl.ds(48, 16))[place]
        return pltpu.make_async_remote_copy(
            src_ref=result.at[which, side, :, rows], dst_ref=land,
            send_sem=fin_send.at[which, place, side], recv_sem=fin_recv.at[which, place, core],
            device_id=at, device_id_type=MESH,
        )

    for which in (1, 0):
        ladder(NR - 1, which)
        h = zl * 4 + (y + which) % 4
        value = jnp.where(lane < counts[h], total[which], 0.0).astype(BF16).reshape(2, 64, BLK)
        for side in range(2):
            result[which, side] = value[:, :, side * 128 : (side + 1) * 128]
        for place in (1, 0):
            for side in range(2):
                if which == 0 and place == 0:
                    @pl.when(core != side)
                    def _():
                        home(0, 0, side).start()
                else:
                    home(which, place, side).start()
    near[0, core] = result[0, core, :, 0:48]

    drain(NR - 1, 0)

    def arrival(which, place, side):
        land = (near, beyond)[place].at[which, side]
        rows = (pl.ds(0, 48), pl.ds(48, 16))[place]
        return pltpu.make_async_remote_copy(
            src_ref=result.at[which, side, :, rows], dst_ref=land,
            send_sem=fin_send.at[which, place, side], recv_sem=fin_recv.at[which, place, side],
            device_id=sibling, device_id_type=MESH,
        )

    for which in range(2):
        for place in range(2):
            for side in range(2):
                if which == 0 and place == 0:
                    @pl.when(core != side)
                    def _():
                        arrival(0, 0, side).wait()
                else:
                    arrival(which, place, side).wait()
    for which in range(2):
        for other in range(2):
            source = (y + ((0, 1), (3, 2))[which][other]) % 4
            for side in range(2):
                out_ref[zl, source, side] = near[which, side, other, 0:32]
                out_ref[1 - zl, source, side, 0:16] = near[which, side, other, 32:48]
                out_ref[1 - zl, source, side, 16:32] = beyond[which, side, other]


def body(amplitudes, cycle_inter, ladder_slab, irrep_counts, slab_irrep):
    any_spec = pl.BlockSpec(memory_space=pl.ANY)
    smem = pl.BlockSpec(memory_space=pltpu.SMEM)
    dma = pltpu.SemaphoreType.DMA
    block = lax.broadcasted_iota(jnp.int32, (3, 8), 1) ^ slab_irrep[0]
    row = lax.broadcasted_iota(jnp.int32, (3, 8), 0)
    table = jnp.where(row == 0, block, jnp.where(row == 1, block >> 2, block & 3))
    out = pl.pallas_call(
        kernel,
        out_shape=jax.ShapeDtypeStruct((2, 4, 2, 32, 128), BF16),
        in_specs=[any_spec, any_spec, any_spec, smem, smem],
        out_specs=pl.BlockSpec(memory_space=pltpu.VMEM),
        scratch_shapes=[
            pltpu.VMEM((32, 32, 2048), BF16),
            pltpu.VMEM((2, 1024, 128), F32),
            pltpu.VMEM((8, 32, 32, BLK), BF16),
        ]
        + [pltpu.VMEM((2, 4, 2, 4, 2, 16, w), BF16) for w in WIDTHS]
        + [
            pltpu.VMEM((2, 4, 32, 32, BLK), BF16),
            pltpu.VMEM((2, 2, 32, 64, BLK), BF16),
            pltpu.VMEM((2, 32, BLK, BLK), BF16),
            pltpu.VMEM((2, 128, BLK), F32),
            pltpu.VMEM((2, 2, 2, 64, 128), BF16),
            pltpu.VMEM((2, 2, 2, 48, 128), BF16),
            pltpu.VMEM((2, 2, 2, 16, 128), BF16),
            dma((5,)),
            dma((3, 18)),
            dma((3, 18)),
            dma((3, 7)),
            dma((3, 7)),
            dma((NR, 4, 3)),
            dma((NR, 4, 3)),
            dma((10,)),
            dma((10,)),
            dma((2, 2, 2)),
            dma((2, 2, 2)),
        ],
        compiler_params=pltpu.CompilerParams(
            collective_id=0, has_side_effects=True, vmem_limit_bytes=56 * 1024 * 1024
        ),
        cost_estimate=pl.CostEstimate(
            flops=11 * 10**9, bytes_accessed=7 * 10**6, transcendentals=0
        ),
    )(amplitudes, cycle_inter.T, ladder_slab, irrep_counts, table)
    return out.reshape(512, 128)


def solution(mesh):
    placed = (
        P(("occ", "vir"), None, None),
        P(None, ("occ", "vir")),
        P(None, None, "vir"),
        P(),
        P(),
    )
    return jax.shard_map(
        body, mesh=mesh, in_specs=placed, out_specs=P("occ", "vir"), check_vma=False
    )
```
